32 devices in a mesh: row: 4 (over y, core), col: 8 (over z, x).
Axes of the slice: x: 2, y: 2, z: 4, core: 2. Of those that a mesh axis runs over, the one named last changes fastest.
Arguments:
- fock_tiles: bfloat16 [256, 15, 128, 128], P(('row', 'col')), may hold values from -6 to 6
- fock_pattern: int32 [256, 15], replicated, may hold values from -1 to 255, as said below
- basis_tiles: bfloat16 [256, 15, 128, 128], P(('row', 'col')), may hold values from -0.25 to 0.25
- basis_pattern: int32 [256, 15], replicated, may hold values from -1 to 255, as said below
- product_pattern: int32 [256, 15], replicated, may hold values from -1 to 255, as said below
- result_pattern: int32 [256, 15], replicated, may hold values from -1 to 255, as said below
- new_index: int32 [256], replicated, may hold values from 0 to 255, as said below
Outputs:
- fock_orth: bfloat16 [256, 15, 128, 128], P(('row', 'col'))
The draws below stay inside these ranges and needn't reach their ends.
Inputs may be any that keep to these rules, and one draw needn't show every extreme that they name: `fock_pattern`: the filled slots of a tile row i come first and hold distinct tile columns within the (16) columns starting at min(max(i - 8, 0), 240); slot 0 holds column i; from 10 to 15 slots of a row are filled, and the rest hold -1. `basis_pattern`: as for fock_pattern. `product_pattern`: as for fock_pattern. `result_pattern`: as for fock_pattern. `new_index`: A permutation; each tile row's new index lies in the same block of 64 consecutive tile rows and has the same remainder modulo 8; the 8 consecutive tile rows starting at a multiple of 8 move into 8 different blocks of 8 rows.
All inputs are finite; a program needn't handle non-finite values.
Results may differ from the reference program's by a relative error of at most 0.0065.
Values may be sent and summed in bfloat16 or wider, within the bound.
No kernel may reach another device: no remote copies, remote signals or barrier semaphores. Data moves between devices by JAX's collectives and lax.ppermute only.
A program may use at most 192 MiB of HBM per device.

```python
import jax
import jax.numpy as jnp
from jax import lax

TILE = 128
RD = 8
H = 8
K = 15
NT = 256
GROUP_ROWS = 64


def banded_pattern(key):
    rows = jnp.arange(NT, dtype=jnp.int32)
    low = jnp.clip(rows - H, 0, NT - 2 * H)
    keys = jax.random.split(jax.random.fold_in(key, 11), NT)
    scores = jax.vmap(lambda one_key: jax.random.permutation(one_key, 2 * H))(keys).astype(jnp.int32)
    spots = jnp.arange(2 * H, dtype=jnp.int32)[None, :]
    scores = jnp.where(spots == (rows - low)[:, None], -1, scores)
    picked = jnp.argsort(scores, axis=1, stable=True)[:, :K].astype(jnp.int32)
    columns = low[:, None] + picked
    regions = NT // 16 + 1
    counts = jax.random.randint(jax.random.fold_in(key, 12), (regions,), 2 * K // 3, K + 1).astype(jnp.int32)
    counts = counts.at[0].set(K)
    counts = counts.at[1].set(2 * K // 3)
    filled = counts[rows // 16]
    slots = jnp.arange(K, dtype=jnp.int32)[None, :]
    return jnp.where(slots < filled[:, None], columns, -1).astype(jnp.int32)


def draw_fock_pattern(key, part):
    return banded_pattern(jax.random.fold_in(key, 101))


def draw_basis_pattern(key, part):
    return banded_pattern(jax.random.fold_in(key, 202))


def draw_product_pattern(key, part):
    return banded_pattern(jax.random.fold_in(key, 303))


def draw_result_pattern(key, part):
    return banded_pattern(jax.random.fold_in(key, 404))


def draw_new_index(key, part):
    groups = NT // GROUP_ROWS
    width = GROUP_ROWS // RD
    keys = jax.random.split(jax.random.fold_in(key, 505), groups)

    def one_group(group_key):
        first_key, second_key, third_key = jax.random.split(group_key, 3)
        outer = jax.random.permutation(first_key, width).astype(jnp.int32)
        inner = jax.random.permutation(second_key, width).astype(jnp.int32)
        shifts = jax.random.permutation(third_key, width).astype(jnp.int32)[:RD]
        source = jnp.arange(width, dtype=jnp.int32)[:, None]
        slot = jnp.arange(RD, dtype=jnp.int32)[None, :]
        target = outer[(inner[source] + shifts[slot]) % width]
        return target * RD + slot
    local = jax.vmap(one_group)(keys)
    bases = jnp.arange(groups, dtype=jnp.int32)[:, None, None] * GROUP_ROWS
    return (local + bases).reshape(NT).astype(jnp.int32)


def steps_of(rng, extent, shards, least, top_value):
    level, own = 1.0, jax.random.fold_in(rng, 6)
    for position, parts in shards:
        steps = jnp.exp(jax.random.uniform(jax.random.fold_in(own, position), (parts,), jnp.float32, least / len(shards), top_value / len(shards)))
        level = level * jnp.repeat(steps, extent[position] // parts).reshape([-1 if axis == position else 1 for axis in range(len(extent))])
    return level


def noise(rng, extent, deviation, most, pieces=(), kind=jnp.bfloat16):
    level = steps_of(rng, extent, pieces, -0.22, 0.18) if pieces else 1.0
    drawn = jax.random.normal(rng, extent, jnp.float32) * deviation * level
    return jnp.minimum(jnp.maximum(drawn, -most), most).astype(kind)


def setup_inputs(seed: int = 0) -> dict:
    streams_of = jax.random.split(jax.random.key(seed), 8)
    fock_tiles = noise(streams_of[0], (NT, K, TILE, TILE), 1.0, 6.0, ((0, 32),))
    fock_pattern = draw_fock_pattern(jax.random.fold_in(streams_of[7], 71), 0)
    basis_tiles = noise(streams_of[2], (NT, K, TILE, TILE), (4 * TILE) ** -0.5, 0.25, ((0, 32),))
    basis_pattern = draw_basis_pattern(jax.random.fold_in(streams_of[7], 71), 0)
    product_pattern = draw_product_pattern(jax.random.fold_in(streams_of[7], 71), 0)
    result_pattern = draw_result_pattern(jax.random.fold_in(streams_of[7], 71), 0)
    new_index = draw_new_index(jax.random.fold_in(streams_of[7], 71), 0)
    return {"fock_tiles": fock_tiles, "fock_pattern": fock_pattern, "basis_tiles": basis_tiles, "basis_pattern": basis_pattern, "product_pattern": product_pattern, "result_pattern": result_pattern, "new_index": new_index}


def reference(fock_tiles, fock_pattern, basis_tiles, basis_pattern, product_pattern, result_pattern, new_index):
    span = 2 * H

    def row_step(accum, row):
        fock_row = fock_tiles[row].astype(jnp.float32)
        fock_cols = fock_pattern[row]
        basis_index = jnp.clip(fock_cols, 0, NT - 1).astype(jnp.int32)
        gathered = basis_tiles[basis_index].astype(jnp.float32)
        gathered_cols = basis_pattern[basis_index]
        prod_cols = product_pattern[row]
        match = (gathered_cols[:, None, :] == prod_cols[None, :, None]) & (prod_cols[None, :, None] >= 0) & (fock_cols[:, None, None] >= 0)
        chosen = jnp.einsum('kps,ksab->kpab', match.astype(jnp.float32), gathered)
        product_row = jnp.einsum('kab,kpbc->pac', fock_row, chosen).astype(jnp.bfloat16)
        basis_row = basis_tiles[row].astype(jnp.float32)
        targets = basis_pattern[row]
        valid = targets >= 0
        target_rows = jnp.clip(targets, 0, NT - 1).astype(jnp.int32)
        result_cols = result_pattern[target_rows]
        second = (prod_cols[None, None, :] == result_cols[:, :, None]) & (result_cols[:, :, None] >= 0) & valid[:, None, None]
        picked = jnp.einsum('srp,pab->srab', second.astype(jnp.float32), product_row.astype(jnp.float32))
        terms = jnp.einsum('sba,srbc->srac', basis_row, picked)
        terms = terms * valid.astype(jnp.float32)[:, None, None, None]
        low = jnp.clip(row - H, 0, NT - span).astype(jnp.int32)
        offsets = jnp.clip(target_rows - low, 0, span - 1).astype(jnp.int32)
        added = jnp.zeros((span,) + terms.shape[1:], jnp.float32).at[offsets].add(terms)
        window = lax.dynamic_slice_in_dim(accum, low, span, 0)
        accum = lax.dynamic_update_slice_in_dim(accum, window + added, low, 0)
        return accum, None

    start = jnp.zeros(fock_tiles.shape, jnp.float32)
    accum, unused = lax.scan(row_step, start, jnp.arange(NT, dtype=jnp.int32))
    orth = accum.astype(jnp.bfloat16)
    return jnp.zeros_like(orth).at[new_index.astype(jnp.int32)].set(orth)
```

```python
import functools

import jax
import jax.numpy as jnp
from jax import lax
from jax.experimental import pallas as pl
from jax.experimental.pallas import tpu as pltpu
from jax.sharding import PartitionSpec as P

H = 8
AXES = ("row", "col")
COST_SCALE = 3_000_000


def layout(rows, cols):
    def place(v):
        g, n = divmod(v, cols)
        return (2 * (g // 2) + n % 2) * cols + 2 * (n // 2) + g % 2

    def beside(v):
        return v + 1 if v % 2 else v - 1

    total = rows * cols
    moved = [place(v) != v for v in range(total)]
    edge = [v % cols in (0, cols - 1) for v in range(total)]
    has_outer = [0 <= beside(v) < total for v in range(total)]
    return {
        "swap": [(v, place(v)) for v in range(total) if moved[v]],
        "mate_a": [(place(v), place(v ^ 1)) for v in range(total) if not moved[v]],
        "mate_b": [(place(v), place(v ^ 1)) for v in range(total) if moved[v]],
        "pair": [(place(v), place(v ^ 1)) for v in range(total)],
        "far_a": [(v, place(beside(v))) for v in range(total) if has_outer[v] and (edge[v] or not moved[v])],
        "far_b": [(place(v), place(beside(v))) for v in range(total) if has_outer[v] and moved[v] and not edge[v]],
        "outer": [(place(v), place(beside(v))) for v in range(total) if has_outer[v]],
        "shifts": [[(place(v), v // cols * cols + (v + s) % cols) for v in range(total)] for s in range(cols)],
    }


BASE, ODD, MOVED, FAR_A = range(4)


def widths(slots, rows, low):
    return [min(slots, 2 * H - 1 - t if low else H + t) for t in range(rows)]


def pack_tables(pattern, base, low, packed_tiles):
    rows, slots = pattern.shape[1:]
    tables = [widths(slots, rows, side) for side in (False, True)]
    width = jnp.where(low[:, None], jnp.array(tables[1]), jnp.array(tables[0]))
    starts = [[sum(table[:t]) for t in range(rows)] for table in tables]
    offset = jnp.where(low[:, None], jnp.array(starts[1]), jnp.array(starts[0]))
    beyond = jnp.where(low[:, None, None], pattern <= base[:, None, None] + H - 2, pattern >= base[:, None, None])
    wanted = (pattern >= 0) & beyond
    earlier = jnp.arange(slots)[None, :] < jnp.arange(slots)[:, None]
    rank = jnp.sum((wanted[:, :, None, :] & earlier).astype(jnp.int32), axis=-1)
    place = jnp.where(wanted & (rank < width[:, :, None]), offset[:, :, None] + rank, -1)
    hit = place.reshape(-1, 1, rows * slots) == jnp.arange(packed_tiles)[None, :, None]
    col_of = jnp.max(jnp.where(hit, pattern.reshape(-1, 1, rows * slots), 0), axis=-1)
    return place, col_of


def spread(pattern, values, origin, span, empty):
    at = pattern[:, :, None] - origin == jnp.arange(span)
    found = jnp.max(jnp.where(at & (pattern >= 0)[:, :, None], values[:, :, None], -1), axis=1)
    return jnp.where(found >= 0, found, empty).astype(jnp.int32)


def either(flag, first, second, act):
    @pl.when(flag != 0)
    def _():
        act(first)

    @pl.when(flag == 0)
    def _():
        act(second)


def tiles_of(ref, row, col, tile):
    return ref.at[pl.ds(pl.multiple_of(row * tile, tile), tile), pl.ds(pl.multiple_of(col * tile, tile), tile)]


def pair_cols(first, count, tile):
    return pl.ds(pl.multiple_of(first * tile, 2 * tile), count * tile)


def pair_rows(first, tile):
    return pl.ds(pl.multiple_of(first * tile, 2 * tile), 2 * tile)


def window(base, rows, r, total):
    low = jnp.clip(base + 2 * r - H, 0, total - 2 * H) - (base - rows)
    return jnp.clip(low // 2 * 2, 0, 3 * rows - 2 * H - 2)


def densify(pool, table, dense, row, count):
    tile = pool.shape[1]

    def one(t, carry):
        for c in range(table.shape[1]):
            dense[pl.ds(pl.multiple_of((row + t) * tile, tile), tile), c * tile : (c + 1) * tile] = pool[table[t, c]]
        return carry

    lax.fori_loop(0, count, one, 0)


def pack_kernel(rows, meta, first, pattern, tiles, packed, held, sem, osem):
    count = tiles.shape[0]
    slots = count // rows
    inward = pltpu.make_async_copy(tiles, held, sem)
    inward.start()
    start = first[0]
    low = first[1] == 0
    tables = [widths(slots, rows, side) for side in (False, True)]
    starts = [[sum(table[:t]) for t in range(rows)] for table in tables]
    inward.wait()
    for t in range(rows):
        offset = jnp.where(low, starts[1][t], starts[0][t])
        end = offset + jnp.where(low, tables[1][t], tables[0][t])

        def one(k, place, t=t, end=end):
            col = pattern[start + t, k]
            take = (col >= 0) & jnp.where(low, col <= start + H - 2, col >= start) & (place < end)

            @pl.when(take)
            def _():
                pltpu.make_async_copy(held.at[t * slots + k], packed.at[place], osem).start()

            return place + take.astype(jnp.int32)

        place = offset
        for k in range(slots):
            place = one(k, place)

        def wait(k, carry):
            pltpu.make_async_copy(held.at[0], packed.at[0], osem).wait()
            return carry

        lax.fori_loop(0, place - offset, wait, 0)


def near_kernel(rows, meta, table, z_home, z_came, mate_a, mate_b, znear, turned_far, turned_own, pool, zd, zf, zo, sem, osem):
    count, tile = z_home.shape[:2]
    odd = meta[ODD]
    own_at = odd * count
    either(meta[MOVED], z_came, z_home, lambda own: pltpu.make_async_copy(own, pool.at[pl.ds(own_at, count)], sem).start())
    either(meta[MOVED], mate_a, mate_b, lambda mate: pltpu.make_async_copy(mate, pool.at[pl.ds(count - own_at, count)], sem).start())
    pool[2 * count] = jnp.zeros(pool.shape[1:], pool.dtype)
    for _ in range(2):
        pltpu.make_async_copy(z_home, z_home, sem).wait()
    densify(pool, table, zd, 0, 2 * rows)
    copies = [pltpu.make_async_copy(zd, znear, osem.at[0])]
    copies[0].start()
    own_rows = pl.ds(pl.multiple_of(odd * rows * tile, rows * tile), rows * tile)

    def far_one(i, carry):
        at = pl.ds(pl.multiple_of((odd * 2 * rows + i) * tile, tile), tile)
        zf[pl.ds(pl.multiple_of(i * tile, tile), tile), :] = zd[own_rows, at].T
        return carry

    def own_one(i, carry):
        at = pl.ds(pl.multiple_of((rows + i) * tile, tile), tile)
        zo[pl.ds(pl.multiple_of(i * tile, tile), tile), :] = zd[:, at].T
        return carry

    lax.fori_loop(0, rows, far_one, 0)
    lax.fori_loop(0, rows, own_one, 0)
    copies += [pltpu.make_async_copy(zf, turned_far, osem.at[1]), pltpu.make_async_copy(zo, turned_own, osem.at[2])]
    copies[1].start()
    copies[2].start()
    for copy in copies:
        copy.wait()


def product_kernel(
    total, rows, meta, ftab, ztab, keep, col_of, f_home, f_came, far_a, far_b, znear, turned,
    prod, lent, packed, fd, zd, pd, zt, fpool, zpool, part, fsem, zsem, tsem, nsem, psem, osem,
):
    count, tile = f_home.shape[:2]
    span, wide = 3 * rows, 2 * H + 2
    base, odd = meta[BASE], meta[ODD]
    far_row = jnp.where(odd == 0, 0, 2 * rows)
    near_rows = pl.ds(pl.multiple_of(rows * tile * (1 - odd), rows * tile), 2 * rows * tile)
    either(meta[MOVED], f_came, f_home, lambda fock: pltpu.make_async_copy(fock, fpool.at[:count], fsem).start())
    either(meta[FAR_A], far_a, far_b, lambda far: pltpu.make_async_copy(far, zpool.at[: far.shape[0]], zsem).start())
    near_in = pltpu.make_async_copy(znear, zd.at[near_rows], nsem)
    near_in.start()
    turn_in = pltpu.make_async_copy(turned, zt, tsem)
    turn_in.start()
    fpool[count] = jnp.zeros(fpool.shape[1:], fpool.dtype)
    zpool[far_a.shape[0]] = jnp.zeros(zpool.shape[1:], zpool.dtype)

    def clear(i, carry):
        pd[pl.ds(pl.multiple_of(i * tile, tile), tile), :] = jnp.zeros((tile, pd.shape[1]), pd.dtype)
        return carry

    lax.fori_loop(0, rows, clear, 0)
    pltpu.make_async_copy(f_home, fpool.at[:count], fsem).wait()
    densify(fpool, ftab, fd, 0, rows)
    pltpu.make_async_copy(far_a, zpool.at[: far_a.shape[0]], zsem).wait()
    densify(zpool, ztab, zd, far_row, rows)
    near_in.wait()
    step = 6 if wide % 6 == 0 else 2
    for r in range(rows // 2):
        k0 = window(base, rows, r, total)
        kcols = pair_cols(k0, wide, tile)

        def block(nb, carry, r=r, k0=k0, kcols=kcols):
            first = k0 + step * nb
            acc = jnp.dot(
                fd[2 * r * tile : (2 * r + 2) * tile, kcols],
                zd[kcols, pair_cols(first, step, tile)],
                preferred_element_type=jnp.float32,
            )
            for i in range(2):
                for j in range(step):
                    piece = acc[i * tile : (i + 1) * tile, j * tile : (j + 1) * tile]
                    piece = jnp.where(keep[2 * r + i, first + j] != 0, piece, 0.0)
                    tiles_of(pd, 2 * r + i, first + j, tile)[...] = piece.astype(pd.dtype)
            return carry

        lax.fori_loop(0, wide // step, block, 0)
    lent_cols = pl.ds(pl.multiple_of((1 - odd) * rows * tile, rows * tile), 2 * rows * tile)
    writes = [pltpu.make_async_copy(pd, prod, psem.at[0]), pltpu.make_async_copy(pd.at[:, lent_cols], lent, psem.at[1])]
    for write in writes:
        write.start()
    turn_in.wait()
    start = jnp.where(odd == 0, 0, rows)
    pairs = rows // 2
    for m in range(pairs):
        r = jnp.where(odd == 0, m, pairs - 1 - m)
        deep = 2 * (m + 1) * tile
        k_at = pl.ds(pl.multiple_of(jnp.where(odd == 0, 0, rows * tile - deep), 2 * tile), deep)
        n_wide = H + 2 * (m + 1)
        n_at = jnp.where(odd == 0, 0, 2 * H - n_wide)
        acc = jnp.dot(
            zt[pair_rows(2 * r, tile), k_at],
            pd[k_at, pair_cols(start + n_at, n_wide, tile)],
            preferred_element_type=jnp.float32,
        )
        part[pair_rows(2 * r, tile), pair_cols(n_at, n_wide, tile)] = acc.astype(part.dtype)
    low_rows = [t for t, w in enumerate(widths(count // rows, rows, True)) for _ in range(w)]
    high_rows = [t for t, w in enumerate(widths(count // rows, rows, False)) for _ in range(w)]
    for p in range(packed.shape[0]):
        t = jnp.where(odd == 1, low_rows[p], high_rows[p])
        pltpu.make_async_copy(tiles_of(part, t, col_of[p], tile), packed.at[p], osem).start()
    pltpu.make_async_copy(packed, packed, osem).wait()
    for write in writes:
        write.wait()


def own_kernel(total, rows, meta, col_of, turned, prod, lent, near, zt, pd, acc_ref, out, sem, osem):
    count, tile = near.shape[:2]
    slots = count // rows
    base, odd = meta[BASE], meta[ODD]
    wide = 2 * H + 2
    own = rows * tile

    def part(index, n):
        return pl.ds(pl.multiple_of(index * own, own), n * own)

    copies = [
        pltpu.make_async_copy(turned, zt, sem.at[0]),
        pltpu.make_async_copy(prod, pd.at[part(odd, 1)], sem.at[1]),
        pltpu.make_async_copy(lent, pd.at[part(1 - odd, 1), part(1 - odd, 2)], sem.at[2]),
    ]
    for copy in copies:
        copy.start()
    pd[part(1 - odd, 1), part(2 * odd, 1)] = jnp.zeros((own, own), pd.dtype)
    acc_ref[:, 3 * own :] = jnp.zeros((own, tile), acc_ref.dtype)
    for copy in copies:
        copy.wait()
    step = 6 if wide % 6 == 0 else 2
    for r in range(rows // 2):
        k0 = window(base, rows, r, total)

        def block(nb, carry, r=r, k0=k0):
            cols = pair_cols(k0 + step * nb, step, tile)
            acc = jnp.dot(zt[2 * r * tile : (2 * r + 2) * tile, :], pd[:, cols], preferred_element_type=jnp.float32)
            acc_ref[2 * r * tile : (2 * r + 2) * tile, cols] = acc.astype(acc_ref.dtype)
            return carry

        lax.fori_loop(0, wide // step, block, 0)

    def one(t, carry):
        for s in range(slots):
            out[t * slots + s] = tiles_of(acc_ref, t, col_of[t, s], tile)[...]
        return carry

    lax.fori_loop(0, rows, one, 0)
    outward = pltpu.make_async_copy(out, near, osem)
    outward.start()
    outward.wait()


def join_kernel(rows, place, where, near, far, *rest):
    outs, (a, b, out, sem, far_sem, osem) = rest[:-6], rest[-6:]
    slots = near.shape[0] // rows
    tiles = far.shape[0]
    inward = pltpu.make_async_copy(far, b.at[:tiles], far_sem)
    inward.start()
    copies = [pltpu.make_async_copy(near.at[pl.ds(where[n] * slots, slots)], a.at[n], sem.at[n]) for n in range(len(outs))]
    for copy in copies:
        copy.start()
    b[tiles] = jnp.zeros(b.shape[1:], b.dtype)
    inward.wait()
    for n, target in enumerate(outs):
        row = where[n]
        copies[n].wait()
        for s in range(slots):
            out[n, s] = (a[n, s].astype(jnp.float32) + b[place[row, s]].astype(jnp.float32)).astype(out.dtype)
        pltpu.make_async_copy(out.at[n], target, osem.at[n]).start()
    for n, target in enumerate(outs):
        pltpu.make_async_copy(out.at[n], target, osem.at[n]).wait()


def gather_kernel(slot, present, *rest):
    parts, (out, held, isem, osem) = rest[:-4], rest[-4:]
    for s, part in enumerate(parts):
        pltpu.make_async_copy(part, held.at[s], isem.at[s]).start()
    for s, part in enumerate(parts):
        pltpu.make_async_copy(part, held.at[s], isem.at[s]).wait()

        @pl.when(present[s] != 0)
        def _(s=s):
            pltpu.make_async_copy(held.at[s], out.at[slot[s]], osem).start()

    pltpu.make_async_copy(out, out, osem).wait()


def call(kernel, scalars, arrays, outs, scratch, name=None, limit=60, cost=1.0):
    any_spec = pl.BlockSpec(memory_space=pl.ANY)
    smem = pl.BlockSpec(memory_space=pltpu.SMEM)
    return pl.pallas_call(
        kernel,
        in_specs=[smem] * len(scalars) + [any_spec] * len(arrays),
        out_specs=[any_spec] * len(outs),
        out_shape=outs,
        scratch_shapes=scratch,
        compiler_params=pltpu.CompilerParams(vmem_limit_bytes=limit * 1024 * 1024),
        cost_estimate=pl.CostEstimate(flops=0, bytes_accessed=int(cost * COST_SCALE), transcendentals=0),
        name=name,
    )(*scalars, *arrays)


def body(fock_tiles, fock_pattern, basis_tiles, basis_pattern, product_pattern, result_pattern, new_index):
    rows, slots, tile = fock_tiles.shape[:3]
    total = fock_pattern.shape[0]
    count = rows * slots
    count_rows, count_cols = lax.axis_size("row"), lax.axis_size("col")
    plan = layout(count_rows, count_cols)
    my_row, my_col = lax.axis_index("row"), lax.axis_index("col")
    group = 2 * (my_row // 2) + my_col % 2
    number = 2 * (my_col // 2) + my_row % 2
    block = group * count_cols + number
    base = block * rows
    odd = number % 2
    moved = (my_row + my_col) % 2
    at_edge = (number == 0) | (number == count_cols - 1)
    home = (my_row * count_cols + my_col) * rows
    meta = jnp.stack([jnp.asarray(m, jnp.int32) for m in (base, odd, moved, (moved == 1) | at_edge)])
    dtype = fock_tiles.dtype
    packed_tiles = max(sum(widths(slots, rows, side)) for side in (False, True))
    span = 3 * rows

    framed = jnp.pad(
        jnp.concatenate([basis_pattern, result_pattern, fock_pattern, product_pattern], axis=1),
        ((rows, rows), (0, 0)),
        constant_values=-1,
    )
    near = lax.dynamic_slice_in_dim(framed, base, span, 0)
    zpat, rpat, fpat, ppat = (near[:, i * slots : (i + 1) * slots] for i in range(4))
    mid = slice(rows, 2 * rows)
    far_side = jnp.where(odd == 0, jnp.concatenate([zpat, rpat], 1)[:rows], jnp.concatenate([zpat, rpat], 1)[2 * rows :])
    far_base = jnp.where(odd == 0, base - rows, base + rows)
    place, col_of = pack_tables(
        jnp.stack([far_side[:, :slots], far_side[:, slots:], rpat[mid]]),
        jnp.stack([far_base, far_base, base]),
        jnp.stack([odd == 1, odd == 1, odd == 0]),
        packed_tiles,
    )
    origin = base - rows
    slot_ids = jnp.arange(2 * count, dtype=jnp.int32).reshape(2 * rows, slots)
    znear_pat = jnp.where(odd == 0, zpat[rows:], zpat[: 2 * rows])
    near_table = spread(znear_pat, slot_ids, origin, span, 2 * count)
    fock_table = spread(fpat[mid], slot_ids[:rows], origin, span, count)
    far_table = spread(far_side[:, :slots], place[0], origin, span, packed_tiles)
    keep = spread(ppat[mid], jnp.ones((rows, slots), jnp.int32), origin, span, 0)
    far_start = jnp.where(odd == 0, 0, rows)
    far_cols = jnp.clip(col_of[1] - origin - far_start, 0, 2 * H - 1)
    own_cols = jnp.where(rpat[mid] >= 0, rpat[mid] - origin, span)
    own_place = jnp.where(place[2] >= 0, place[2], packed_tiles)

    def permute(x, name):
        return lax.ppermute(x, AXES, plan[name])

    def dense(n_rows, n_cols, kind=dtype):
        return pltpu.VMEM((n_rows * tile, n_cols * tile), kind)

    def pool(n):
        return pltpu.VMEM((n, tile, tile), dtype)

    def shape(*dims):
        return jax.ShapeDtypeStruct(dims, dtype)

    dma = pltpu.SemaphoreType.DMA
    packed_shape = shape(packed_tiles, tile, tile)
    block_shape = shape(count, tile, tile)
    z_home, f_home = basis_tiles.reshape(count, tile, tile), fock_tiles.reshape(count, tile, tile)

    def pack(first, tiles):
        kernel = functools.partial(pack_kernel, rows)
        scalars = [meta, jnp.stack([jnp.asarray(f, jnp.int32) for f in first]), basis_pattern]
        return call(kernel, scalars, [tiles], [packed_shape], [pool(count), dma, dma], name="pack", limit=8, cost=5)[0]

    z_came = permute(z_home, "swap")
    mate_a = permute(z_home, "mate_a")
    far_a = permute(pack((home, my_col % 2), z_home), "far_a")
    f_came = permute(f_home, "swap")
    z_came, far_a = lax.optimization_barrier((z_came, far_a))
    far_b = permute(pack((base, odd), z_came), "far_b")
    mate_b = permute(z_came, "mate_b")
    znear, turned_far, turned_own = call(
        functools.partial(near_kernel, rows),
        [meta, near_table],
        [z_home, z_came, mate_a, mate_b],
        [shape(2 * rows * tile, span * tile), shape(rows * tile, rows * tile), shape(rows * tile, 2 * rows * tile)],
        [pool(2 * count + 1), dense(2 * rows, span), dense(rows, rows), dense(rows, 2 * rows), dma, dma((3,))],
        name="near",
        limit=40,
        cost=14,
    )
    prod, lent, packed = call(
        functools.partial(product_kernel, total, rows),
        [meta, fock_table, far_table, keep, far_cols],
        [f_home, f_came, far_a, far_b, znear, turned_far],
        [shape(rows * tile, span * tile), shape(rows * tile, 2 * rows * tile), packed_shape],
        [dense(rows, span), dense(span, span), dense(rows, span), dense(rows, rows)]
        + [pool(count + 1), pool(packed_tiles + 1), dense(rows, 2 * H)]
        + [dma] * 4
        + [dma((2,)), dma],
        name="product",
        cost=27,
    )
    far = permute(packed, "outer")
    lent = permute(lent, "pair")
    (near_sum,) = call(
        functools.partial(own_kernel, total, rows),
        [meta, own_cols],
        [turned_own, prod, lent],
        [block_shape],
        [dense(rows, 2 * rows), dense(2 * rows, span), dense(rows, span + 1), pool(count), dma((3,)), dma],
        name="own",
        limit=40,
        cost=20,
    )
    shift = (lax.dynamic_slice_in_dim(new_index, base, rows, 0) // rows - number) % count_cols
    hit = shift[None, :] == jnp.arange(count_cols, dtype=jnp.int32)[:, None]
    where = jnp.sum(hit.astype(jnp.int32) * jnp.arange(rows, dtype=jnp.int32)[None, :], axis=1)
    outs = call(
        functools.partial(join_kernel, rows),
        [own_place, where],
        [near_sum, far],
        [shape(slots, tile, tile)] * count_cols,
        [pltpu.VMEM((count_cols, slots, tile, tile), dtype), pool(packed_tiles + 1), pltpu.VMEM((count_cols, slots, tile, tile), dtype)]
        + [dma((count_cols,)), dma, dma((count_cols,))],
        name="join",
        limit=24,
        cost=5,
    )
    parts = [lax.ppermute(out, AXES, plan["shifts"][s]) for s, out in enumerate(outs)]
    wanted = home + jnp.arange(rows, dtype=jnp.int32)
    found = new_index[None, :] == wanted[:, None]
    anchor = jnp.sum(found.astype(jnp.int32) * jnp.arange(total, dtype=jnp.int32)[None, :], axis=1)
    came = (my_col - anchor // rows) % count_cols
    hit = came[None, :] == jnp.arange(count_cols, dtype=jnp.int32)[:, None]
    slot = jnp.sum(hit.astype(jnp.int32) * jnp.arange(rows, dtype=jnp.int32)[None, :], axis=1)
    present = jnp.sum(hit.astype(jnp.int32), axis=1)
    (out,) = call(
        gather_kernel,
        [slot, present],
        parts,
        [shape(rows, slots, tile, tile)],
        [pltpu.VMEM((count_cols, slots, tile, tile), dtype), dma((count_cols,)), dma],
        name="gather",
        limit=16,
        cost=4,
    )
    return out


def solution(mesh):
    placed = P(AXES, None, None, None)
    return jax.shard_map(
        body,
        mesh=mesh,
        in_specs=(placed, P(), placed, P(), P(), P(), P()),
        out_specs=placed,
        check_vma=False,
    )
```

```python
import functools

import jax
import jax.numpy as jnp
from jax import lax
from jax.experimental import pallas as pl
from jax.experimental.pallas import tpu as pltpu
from jax.sharding import PartitionSpec as P

H = 8
AXES = ("row", "col")
COST_SCALE = 3_000_000


def layout(rows, cols):
    def place(v):
        g, n = divmod(v, cols)
        return (2 * (g // 2) + n % 2) * cols + 2 * (n // 2) + g % 2

    def beside(v):
        return v + 1 if v % 2 else v - 1

    total = rows * cols
    moved = [place(v) != v for v in range(total)]
    edge = [v % cols in (0, cols - 1) for v in range(total)]
    has_outer = [0 <= beside(v) < total for v in range(total)]
    return {
        "swap": [(v, place(v)) for v in range(total) if moved[v]],
        "mate_a": [(place(v), place(v ^ 1)) for v in range(total) if not moved[v]],
        "mate_b": [(place(v), place(v ^ 1)) for v in range(total) if moved[v]],
        "pair": [(place(v), place(v ^ 1)) for v in range(total)],
        "far_a": [(v, place(beside(v))) for v in range(total) if has_outer[v] and moved[v] == edge[v]],
        "far_b": [(place(v), place(beside(v))) for v in range(total) if has_outer[v] and moved[v] and not edge[v]],
        "far_c": [(v, place(beside(v))) for v in range(total) if has_outer[v] and edge[v] and not moved[v]],
        "outer": [(place(v), place(beside(v))) for v in range(total) if has_outer[v]],
        "shifts": [[(place(v), v // cols * cols + (v + s) % cols) for v in range(total)] for s in range(cols)],
    }


BASE, ODD, MOVED, FAR = range(4)


def widths(slots, rows, low):
    return [min(slots, 2 * H - 1 - t if low else H + t) for t in range(rows)]


def pack_tables(pattern, base, low, packed_tiles):
    rows, slots = pattern.shape[1:]
    tables = [widths(slots, rows, side) for side in (False, True)]
    width = jnp.where(low[:, None], jnp.array(tables[1]), jnp.array(tables[0]))
    starts = [[sum(table[:t]) for t in range(rows)] for table in tables]
    offset = jnp.where(low[:, None], jnp.array(starts[1]), jnp.array(starts[0]))
    beyond = jnp.where(low[:, None, None], pattern <= base[:, None, None] + H - 2, pattern >= base[:, None, None])
    wanted = (pattern >= 0) & beyond
    earlier = jnp.arange(slots)[None, :] < jnp.arange(slots)[:, None]
    rank = jnp.sum((wanted[:, :, None, :] & earlier).astype(jnp.int32), axis=-1)
    place = jnp.where(wanted & (rank < width[:, :, None]), offset[:, :, None] + rank, -1)
    hit = place.reshape(-1, 1, rows * slots) == jnp.arange(packed_tiles)[None, :, None]
    col_of = jnp.max(jnp.where(hit, pattern.reshape(-1, 1, rows * slots), 0), axis=-1)
    return place, col_of


def spread(pattern, values, origin, span, empty):
    at = pattern[:, :, None] - origin == jnp.arange(span)
    found = jnp.max(jnp.where(at & (pattern >= 0)[:, :, None], values[:, :, None], -1), axis=1)
    return jnp.where(found >= 0, found, empty).astype(jnp.int32)


def either(flag, first, second, act):
    @pl.when(flag != 0)
    def _():
        act(first)

    @pl.when(flag == 0)
    def _():
        act(second)


def tiles_of(ref, row, col, tile):
    return ref.at[pl.ds(pl.multiple_of(row * tile, tile), tile), pl.ds(pl.multiple_of(col * tile, tile), tile)]


def pair_cols(first, count, tile):
    return pl.ds(pl.multiple_of(first * tile, 2 * tile), count * tile)


def pair_rows(first, tile):
    return pl.ds(pl.multiple_of(first * tile, 2 * tile), 2 * tile)


def window(base, rows, r, total):
    low = jnp.clip(base + 2 * r - H, 0, total - 2 * H) - (base - rows)
    return jnp.clip(low // 2 * 2, 0, 3 * rows - 2 * H - 2)


def densify(pool, table, dense, row, count):
    tile = pool.shape[1]

    def one(t, carry):
        for c in range(table.shape[1]):
            dense[pl.ds(pl.multiple_of((row + t) * tile, tile), tile), c * tile : (c + 1) * tile] = pool[table[t, c]]
        return carry

    lax.fori_loop(0, count, one, 0)


def pack_kernel(rows, first, pattern, tiles, packed, held, table, sem):
    count = tiles.shape[0]
    slots = count // rows
    inward = pltpu.make_async_copy(tiles, held, sem)
    inward.start()
    start = first[0]
    low = first[1] == 0
    trash = packed.shape[0]
    for p in range(trash):
        table[p] = 0
    tables = [widths(slots, rows, side) for side in (False, True)]
    starts = [[sum(table[:t]) for t in range(rows)] for table in tables]
    for t in range(rows):
        place = jnp.where(low, starts[1][t], starts[0][t])
        end = place + jnp.where(low, tables[1][t], tables[0][t])
        for k in range(slots):
            col = pattern[start + t, k]
            take = (col >= 0) & jnp.where(low, col <= start + H - 2, col >= start) & (place < end)
            table[jnp.where(take, place, trash)] = t * slots + k
            place = place + take.astype(jnp.int32)
    inward.wait()
    for p in range(trash):
        packed[p] = held[table[p]]


def near_kernel(rows, meta, table, z_home, z_came, mate_a, mate_b, znear, turned_far, turned_own, pool, zd, zf, zo, sem, osem):
    count, tile = z_home.shape[:2]
    odd = meta[ODD]
    own_at = odd * count
    either(meta[MOVED], z_came, z_home, lambda own: pltpu.make_async_copy(own, pool.at[pl.ds(own_at, count)], sem).start())
    either(meta[MOVED], mate_a, mate_b, lambda mate: pltpu.make_async_copy(mate, pool.at[pl.ds(count - own_at, count)], sem).start())
    pool[2 * count] = jnp.zeros(pool.shape[1:], pool.dtype)
    for _ in range(2):
        pltpu.make_async_copy(z_home, z_home, sem).wait()
    densify(pool, table, zd, 0, 2 * rows)
    copies = [pltpu.make_async_copy(zd, znear, osem.at[0])]
    copies[0].start()
    own_rows = pl.ds(pl.multiple_of(odd * rows * tile, rows * tile), rows * tile)

    def far_one(i, carry):
        at = pl.ds(pl.multiple_of((odd * 2 * rows + i) * tile, tile), tile)
        zf[pl.ds(pl.multiple_of(i * tile, tile), tile), :] = zd[own_rows, at].T
        return carry

    def own_one(i, carry):
        at = pl.ds(pl.multiple_of((rows + i) * tile, tile), tile)
        zo[pl.ds(pl.multiple_of(i * tile, tile), tile), :] = zd[:, at].T
        return carry

    lax.fori_loop(0, rows, far_one, 0)
    lax.fori_loop(0, rows, own_one, 0)
    copies += [pltpu.make_async_copy(zf, turned_far, osem.at[1]), pltpu.make_async_copy(zo, turned_own, osem.at[2])]
    copies[1].start()
    copies[2].start()
    for copy in copies:
        copy.wait()


def product_kernel(
    total, rows, meta, ftab, ztab, keep, col_of, f_home, f_came, far_a, far_b, far_c, znear, turned,
    prod, lent_0, lent_1, packed, fd, zd, pd, zt, fpool, zpool, part, fsem, zsem, tsem, nsem, psem, osem,
):
    count, tile = f_home.shape[:2]
    span, wide = 3 * rows, 2 * H + 2
    base, odd = meta[BASE], meta[ODD]
    far_row = jnp.where(odd == 0, 0, 2 * rows)
    near_rows = pl.ds(pl.multiple_of(rows * tile * (1 - odd), rows * tile), 2 * rows * tile)
    either(meta[MOVED], f_came, f_home, lambda fock: pltpu.make_async_copy(fock, fpool.at[:count], fsem).start())
    for kind, far in enumerate((far_b, far_a, far_c)):

        @pl.when(meta[FAR] == kind)
        def _(far=far):
            pltpu.make_async_copy(far, zpool.at[: far.shape[0]], zsem).start()

    near_in = pltpu.make_async_copy(znear, zd.at[near_rows], nsem)
    near_in.start()
    turn_in = pltpu.make_async_copy(turned, zt, tsem)
    turn_in.start()
    fpool[count] = jnp.zeros(fpool.shape[1:], fpool.dtype)
    zpool[far_a.shape[0]] = jnp.zeros(zpool.shape[1:], zpool.dtype)

    def clear(i, carry):
        pd[pl.ds(pl.multiple_of(i * tile, tile), tile), :] = jnp.zeros((tile, pd.shape[1]), pd.dtype)
        return carry

    lax.fori_loop(0, rows, clear, 0)
    pltpu.make_async_copy(f_home, fpool.at[:count], fsem).wait()
    densify(fpool, ftab, fd, 0, rows)
    pltpu.make_async_copy(far_a, zpool.at[: far_a.shape[0]], zsem).wait()
    densify(zpool, ztab, zd, far_row, rows)
    near_in.wait()
    step = 6 if wide % 6 == 0 else 2
    for r in range(rows // 2):
        k0 = window(base, rows, r, total)
        kcols = pair_cols(k0, wide, tile)

        def block(nb, carry, r=r, k0=k0, kcols=kcols):
            first = k0 + step * nb
            acc = jnp.dot(
                fd[2 * r * tile : (2 * r + 2) * tile, kcols],
                zd[kcols, pair_cols(first, step, tile)],
                preferred_element_type=jnp.float32,
            )
            for i in range(2):
                for j in range(step):
                    piece = acc[i * tile : (i + 1) * tile, j * tile : (j + 1) * tile]
                    piece = jnp.where(keep[2 * r + i, first + j] != 0, piece, 0.0)
                    tiles_of(pd, 2 * r + i, first + j, tile)[...] = piece.astype(pd.dtype)
            return carry

        lax.fori_loop(0, wide // step, block, 0)
    writes = [pltpu.make_async_copy(pd, prod, psem.at[0])]
    for i, lent in enumerate((lent_0, lent_1)):
        cols = pl.ds(pl.multiple_of((1 - odd + i) * rows * tile, rows * tile), rows * tile)
        writes.append(pltpu.make_async_copy(pd.at[:, cols], lent, psem.at[1 + i]))
    for write in writes:
        write.start()
    turn_in.wait()
    start = jnp.where(odd == 0, 0, rows)
    pairs = rows // 2
    for m in range(pairs):
        r = jnp.where(odd == 0, m, pairs - 1 - m)
        deep = 2 * (m + 1) * tile
        k_at = pl.ds(pl.multiple_of(jnp.where(odd == 0, 0, rows * tile - deep), 2 * tile), deep)
        n_wide = H + 2 * (m + 1)
        n_at = jnp.where(odd == 0, 0, 2 * H - n_wide)
        acc = jnp.dot(
            zt[pair_rows(2 * r, tile), k_at],
            pd[k_at, pair_cols(start + n_at, n_wide, tile)],
            preferred_element_type=jnp.float32,
        )
        part[pair_rows(2 * r, tile), pair_cols(n_at, n_wide, tile)] = acc.astype(part.dtype)
    low_rows = [t for t, w in enumerate(widths(count // rows, rows, True)) for _ in range(w)]
    high_rows = [t for t, w in enumerate(widths(count // rows, rows, False)) for _ in range(w)]
    for p in range(packed.shape[0]):
        t = jnp.where(odd == 1, low_rows[p], high_rows[p])
        pltpu.make_async_copy(tiles_of(part, t, col_of[p], tile), packed.at[p], osem).start()
    pltpu.make_async_copy(packed, packed, osem).wait()
    for write in writes:
        write.wait()


def own_kernel(total, rows, meta, col_of, turned, prod, lent_0, lent_1, near, zt, pd, acc_ref, out, sem, osem):
    count, tile = near.shape[:2]
    slots = count // rows
    base, odd = meta[BASE], meta[ODD]
    wide = 2 * H + 2
    own = rows * tile

    def part(index, n):
        return pl.ds(pl.multiple_of(index * own, own), n * own)

    copies = [
        pltpu.make_async_copy(turned, zt, sem.at[0]),
        pltpu.make_async_copy(prod, pd.at[part(odd, 1)], sem.at[1]),
        pltpu.make_async_copy(lent_0, pd.at[part(1 - odd, 1), part(1 - odd, 1)], sem.at[2]),
        pltpu.make_async_copy(lent_1, pd.at[part(1 - odd, 1), part(2 - odd, 1)], sem.at[3]),
    ]
    for copy in copies:
        copy.start()
    pd[part(1 - odd, 1), part(2 * odd, 1)] = jnp.zeros((own, own), pd.dtype)
    acc_ref[:, 3 * own :] = jnp.zeros((own, tile), acc_ref.dtype)
    for copy in copies:
        copy.wait()
    step = 6 if wide % 6 == 0 else 2
    for r in range(rows // 2):
        k0 = window(base, rows, r, total)

        def block(nb, carry, r=r, k0=k0):
            cols = pair_cols(k0 + step * nb, step, tile)
            acc = jnp.dot(zt[2 * r * tile : (2 * r + 2) * tile, :], pd[:, cols], preferred_element_type=jnp.float32)
            acc_ref[2 * r * tile : (2 * r + 2) * tile, cols] = acc.astype(acc_ref.dtype)
            return carry

        lax.fori_loop(0, wide // step, block, 0)

    def one(t, carry):
        for s in range(slots):
            out[t * slots + s] = tiles_of(acc_ref, t, col_of[t, s], tile)[...]
        return carry

    lax.fori_loop(0, rows, one, 0)
    outward = pltpu.make_async_copy(out, near, osem)
    outward.start()
    outward.wait()


def join_kernel(rows, place, where, near, far, *rest):
    outs = rest
    slots = near.shape[0] // rows
    tiles = far.shape[0]
    for n, out in enumerate(outs):
        row = where[n]

        def one(s, carry, out=out, row=row):
            at = place[row, s]

            @pl.when(at < tiles)
            def _():
                out[s] = near[row * slots + s] + far[at]

            @pl.when(at >= tiles)
            def _():
                out[s] = near[row * slots + s]

            return carry

        lax.fori_loop(0, slots, one, 0)


def gather_kernel(slot, present, *rest):
    parts, (out, sem) = rest[:-2], rest[-2:]
    for s, part in enumerate(parts):

        @pl.when(present[s] != 0)
        def _(s=s, part=part):
            pltpu.make_async_copy(part, out.at[slot[s]], sem).start()

    pltpu.make_async_copy(out, out, sem).wait()


def call(kernel, scalars, arrays, outs, scratch, name=None, limit=60, cost=1.0, held_in=False, held_out=False):
    any_spec = pl.BlockSpec(memory_space=pl.ANY)
    smem = pl.BlockSpec(memory_space=pltpu.SMEM)
    vmem = pl.BlockSpec(memory_space=pltpu.VMEM)
    return pl.pallas_call(
        kernel,
        in_specs=[smem] * len(scalars) + [vmem if held_in else any_spec] * len(arrays),
        out_specs=[vmem if held_out else any_spec] * len(outs),
        out_shape=outs,
        scratch_shapes=scratch,
        compiler_params=pltpu.CompilerParams(vmem_limit_bytes=limit * 1024 * 1024),
        cost_estimate=pl.CostEstimate(flops=0, bytes_accessed=int(cost * COST_SCALE), transcendentals=0),
        name=name,
    )(*scalars, *arrays)


def body(fock_tiles, fock_pattern, basis_tiles, basis_pattern, product_pattern, result_pattern, new_index):
    rows, slots, tile = fock_tiles.shape[:3]
    total = fock_pattern.shape[0]
    count = rows * slots
    count_rows, count_cols = lax.axis_size("row"), lax.axis_size("col")
    plan = layout(count_rows, count_cols)
    my_row, my_col = lax.axis_index("row"), lax.axis_index("col")
    group = 2 * (my_row // 2) + my_col % 2
    number = 2 * (my_col // 2) + my_row % 2
    block = group * count_cols + number
    base = block * rows
    odd = number % 2
    moved = (my_row + my_col) % 2
    at_edge = ((number == 0) | (number == count_cols - 1)).astype(jnp.int32)
    home = (my_row * count_cols + my_col) * rows
    meta = jnp.stack([jnp.asarray(m, jnp.int32) for m in (base, odd, moved, jnp.where(moved == 1, 1, 2 * at_edge))])
    dtype = fock_tiles.dtype
    packed_tiles = max(sum(widths(slots, rows, side)) for side in (False, True))
    span = 3 * rows

    framed = jnp.pad(
        jnp.concatenate([basis_pattern, result_pattern, fock_pattern, product_pattern], axis=1),
        ((rows, rows), (0, 0)),
        constant_values=-1,
    )
    near = lax.dynamic_slice_in_dim(framed, base, span, 0)
    zpat, rpat, fpat, ppat = (near[:, i * slots : (i + 1) * slots] for i in range(4))
    mid = slice(rows, 2 * rows)
    far_side = jnp.where(odd == 0, jnp.concatenate([zpat, rpat], 1)[:rows], jnp.concatenate([zpat, rpat], 1)[2 * rows :])
    far_base = jnp.where(odd == 0, base - rows, base + rows)
    place, col_of = pack_tables(
        jnp.stack([far_side[:, :slots], far_side[:, slots:], rpat[mid]]),
        jnp.stack([far_base, far_base, base]),
        jnp.stack([odd == 1, odd == 1, odd == 0]),
        packed_tiles,
    )
    origin = base - rows
    slot_ids = jnp.arange(2 * count, dtype=jnp.int32).reshape(2 * rows, slots)
    znear_pat = jnp.where(odd == 0, zpat[rows:], zpat[: 2 * rows])
    near_table = spread(znear_pat, slot_ids, origin, span, 2 * count)
    fock_table = spread(fpat[mid], slot_ids[:rows], origin, span, count)
    far_table = spread(far_side[:, :slots], place[0], origin, span, packed_tiles)
    keep = spread(ppat[mid], jnp.ones((rows, slots), jnp.int32), origin, span, 0)
    far_start = jnp.where(odd == 0, 0, rows)
    far_cols = jnp.clip(col_of[1] - origin - far_start, 0, 2 * H - 1)
    own_cols = jnp.where(rpat[mid] >= 0, rpat[mid] - origin, span)
    own_place = jnp.where(place[2] >= 0, place[2], packed_tiles)

    def permute(x, name):
        return lax.ppermute(x, AXES, plan[name])

    def dense(n_rows, n_cols, kind=dtype):
        return pltpu.VMEM((n_rows * tile, n_cols * tile), kind)

    def pool(n):
        return pltpu.VMEM((n, tile, tile), dtype)

    def shape(*dims):
        return jax.ShapeDtypeStruct(dims, dtype)

    dma = pltpu.SemaphoreType.DMA
    packed_shape = shape(packed_tiles, tile, tile)
    block_shape = shape(count, tile, tile)
    z_home, f_home = basis_tiles.reshape(count, tile, tile), fock_tiles.reshape(count, tile, tile)

    def pack(first, tiles):
        kernel = functools.partial(pack_kernel, rows)
        scalars = [jnp.stack([jnp.asarray(f, jnp.int32) for f in first]), basis_pattern]
        scratch = [pool(count), pltpu.SMEM((packed_tiles + 1,), jnp.int32), dma]
        return call(kernel, scalars, [tiles], [packed_shape], scratch, name="pack", limit=12, cost=4, held_out=True)[0]

    z_came = permute(z_home, "swap")
    mate_a = permute(z_home, "mate_a")
    packed_a = pack((home, my_col % 2), z_home)
    far_a = permute(packed_a, "far_a")
    f_came = permute(f_home, "swap")
    z_came, far_a = lax.optimization_barrier((z_came, far_a))
    far_b = permute(pack((base, odd), z_came), "far_b")
    mate_b = permute(z_came, "mate_b")
    znear, turned_far, turned_own = call(
        functools.partial(near_kernel, rows),
        [meta, near_table],
        [z_home, z_came, mate_a, mate_b],
        [shape(2 * rows * tile, span * tile), shape(rows * tile, rows * tile), shape(rows * tile, 2 * rows * tile)],
        [pool(2 * count + 1), dense(2 * rows, span), dense(rows, rows), dense(rows, 2 * rows), dma, dma((3,))],
        name="near",
        limit=40,
        cost=14,
    )
    packed_a, turned_far = lax.optimization_barrier((packed_a, turned_far))
    far_c = permute(packed_a, "far_c")
    prod, lent_0, lent_1, packed = call(
        functools.partial(product_kernel, total, rows),
        [meta, fock_table, far_table, keep, far_cols],
        [f_home, f_came, far_a, far_b, far_c, znear, turned_far],
        [shape(rows * tile, span * tile), shape(rows * tile, rows * tile), shape(rows * tile, rows * tile), packed_shape],
        [dense(rows, span), dense(span, span), dense(rows, span), dense(rows, rows)]
        + [pool(count + 1), pool(packed_tiles + 1), dense(rows, 2 * H)]
        + [dma] * 4
        + [dma((3,)), dma],
        name="product",
        limit=50,
        cost=27,
    )
    far = permute(packed, "outer")
    lent_0, lent_1 = permute(lent_0, "pair"), permute(lent_1, "pair")
    (near_sum,) = call(
        functools.partial(own_kernel, total, rows),
        [meta, own_cols],
        [turned_own, prod, lent_0, lent_1],
        [block_shape],
        [dense(rows, 2 * rows), dense(2 * rows, span), dense(rows, span + 1), pool(count), dma((4,)), dma],
        name="own",
        limit=40,
        cost=0.1,
    )
    shift = (lax.dynamic_slice_in_dim(new_index, base, rows, 0) // rows - number) % count_cols
    hit = shift[None, :] == jnp.arange(count_cols, dtype=jnp.int32)[:, None]
    where = jnp.sum(hit.astype(jnp.int32) * jnp.arange(rows, dtype=jnp.int32)[None, :], axis=1)
    outs = call(
        functools.partial(join_kernel, rows),
        [own_place, where],
        [near_sum, far],
        [shape(slots, tile, tile)] * count_cols,
        [],
        name="join",
        limit=16,
        cost=4,
        held_in=True,
        held_out=True,
    )
    parts = [lax.ppermute(out, AXES, plan["shifts"][s]) for s, out in enumerate(outs)]
    wanted = home + jnp.arange(rows, dtype=jnp.int32)
    found = new_index[None, :] == wanted[:, None]
    anchor = jnp.sum(found.astype(jnp.int32) * jnp.arange(total, dtype=jnp.int32)[None, :], axis=1)
    came = (my_col - anchor // rows) % count_cols
    hit = came[None, :] == jnp.arange(count_cols, dtype=jnp.int32)[:, None]
    slot = jnp.sum(hit.astype(jnp.int32) * jnp.arange(rows, dtype=jnp.int32)[None, :], axis=1)
    present = jnp.sum(hit.astype(jnp.int32), axis=1)
    (out,) = call(
        gather_kernel,
        [slot, present],
        parts,
        [shape(rows, slots, tile, tile)],
        [dma],
        name="gather",
        limit=16,
        cost=3,
        held_in=True,
    )
    return out


def solution(mesh):
    placed = P(AXES, None, None, None)
    return jax.shard_map(
        body,
        mesh=mesh,
        in_specs=(placed, P(), placed, P(), P(), P(), P()),
        out_specs=placed,
        check_vma=False,
    )
```

```python
import functools

import jax
import jax.numpy as jnp
from jax import lax
from jax.experimental import pallas as pl
from jax.experimental.pallas import tpu as pltpu
from jax.sharding import PartitionSpec as P

H = 8
AXES = ("row", "col")
COST_SCALE = 3_000_000


def layout(rows, cols):
    def place(v):
        g, n = divmod(v, cols)
        return (2 * (g // 2) + n % 2) * cols + 2 * (n // 2) + g % 2

    def beside(v):
        return v + 1 if v % 2 else v - 1

    total = rows * cols
    moved = [place(v) != v for v in range(total)]
    edge = [v % cols in (0, cols - 1) for v in range(total)]
    has_outer = [0 <= beside(v) < total for v in range(total)]
    return {
        "swap": [(v, place(v)) for v in range(total) if moved[v]],
        "mate_a": [(place(v), place(v ^ 1)) for v in range(total) if not moved[v]],
        "mate_b": [(place(v), place(v ^ 1)) for v in range(total) if moved[v]],
        "pair": [(place(v), place(v ^ 1)) for v in range(total)],
        "far_a": [(v, place(beside(v))) for v in range(total) if has_outer[v] and moved[v] == edge[v]],
        "far_b": [(place(v), place(beside(v))) for v in range(total) if has_outer[v] and moved[v] and not edge[v]],
        "far_c": [(v, place(beside(v))) for v in range(total) if has_outer[v] and edge[v] and not moved[v]],
        "outer": [(place(v), place(beside(v))) for v in range(total) if has_outer[v]],
        "shifts": [[(place(v), v // cols * cols + (v + s) % cols) for v in range(total)] for s in range(cols)],
    }


BASE, ODD, MOVED, FAR = range(4)


def widths(slots, rows, low):
    return [min(slots, 2 * H - 1 - t if low else H + t) for t in range(rows)]


def pack_order(rows, low, small_first):
    half = rows // 2
    if low and small_first:
        return [*range(half, rows), *range(half)]
    return list(range(rows))


def pack_starts(slots, rows, low, small_first):
    table, starts, at = widths(slots, rows, low), [0] * rows, 0
    for t in pack_order(rows, low, small_first):
        starts[t] = at
        at += table[t]
    return starts


def pack_tables(pattern, base, low, small_first, packed_tiles):
    rows, slots = pattern.shape[1:]
    width = jnp.where(low[:, None], jnp.array(widths(slots, rows, True)), jnp.array(widths(slots, rows, False)))
    starts = [jnp.array([pack_starts(slots, rows, side, first) for first in small_first]) for side in (False, True)]
    offset = jnp.where(low[:, None], starts[1], starts[0])
    beyond = jnp.where(low[:, None, None], pattern <= base[:, None, None] + H - 2, pattern >= base[:, None, None])
    wanted = (pattern >= 0) & beyond
    earlier = jnp.arange(slots)[None, :] < jnp.arange(slots)[:, None]
    rank = jnp.sum((wanted[:, :, None, :] & earlier).astype(jnp.int32), axis=-1)
    place = jnp.where(wanted & (rank < width[:, :, None]), offset[:, :, None] + rank, -1)
    hit = place.reshape(-1, 1, rows * slots) == jnp.arange(packed_tiles)[None, :, None]
    col_of = jnp.max(jnp.where(hit, pattern.reshape(-1, 1, rows * slots), 0), axis=-1)
    return place, col_of


def spread(pattern, values, origin, span, empty):
    at = pattern[:, :, None] - origin == jnp.arange(span)
    found = jnp.max(jnp.where(at & (pattern >= 0)[:, :, None], values[:, :, None], -1), axis=1)
    return jnp.where(found >= 0, found, empty).astype(jnp.int32)


def either(flag, first, second, act):
    @pl.when(flag != 0)
    def _():
        act(first)

    @pl.when(flag == 0)
    def _():
        act(second)


def tiles_of(ref, row, col, tile):
    return ref.at[pl.ds(pl.multiple_of(row * tile, tile), tile), pl.ds(pl.multiple_of(col * tile, tile), tile)]


def pair_cols(first, count, tile):
    return pl.ds(pl.multiple_of(first * tile, 2 * tile), count * tile)


def pair_rows(first, tile):
    return pl.ds(pl.multiple_of(first * tile, 2 * tile), 2 * tile)


def window(base, rows, r, total):
    low = jnp.clip(base + 2 * r - H, 0, total - 2 * H) - (base - rows)
    return jnp.clip(low // 2 * 2, 0, 3 * rows - 2 * H - 2)


def densify(pool, table, dense, row, count):
    tile = pool.shape[1]

    def one(t, carry):
        for c in range(table.shape[1]):
            dense[pl.ds(pl.multiple_of((row + t) * tile, tile), tile), c * tile : (c + 1) * tile] = pool[table[t, c]]
        return carry

    lax.fori_loop(0, count, one, 0)


def pack_kernel(rows, first, pattern, tiles, packed, held, table, sem):
    count = tiles.shape[0]
    slots = count // rows
    inward = pltpu.make_async_copy(tiles, held, sem)
    inward.start()
    start = first[0]
    low = first[1] == 0
    trash = packed.shape[0]
    for p in range(trash):
        table[p] = 0
    tables = [widths(slots, rows, side) for side in (False, True)]
    starts = [[sum(table[:t]) for t in range(rows)] for table in tables]
    for t in range(rows):
        place = jnp.where(low, starts[1][t], starts[0][t])
        end = place + jnp.where(low, tables[1][t], tables[0][t])
        for k in range(slots):
            col = pattern[start + t, k]
            take = (col >= 0) & jnp.where(low, col <= start + H - 2, col >= start) & (place < end)
            table[jnp.where(take, place, trash)] = t * slots + k
            place = place + take.astype(jnp.int32)
    inward.wait()
    for p in range(trash):
        packed[p] = held[table[p]]


def near_kernel(rows, meta, table, z_home, z_came, mate_a, mate_b, znear, turned_far, turned_own, pool, zd, zf, zo, sem, osem):
    count, tile = z_home.shape[:2]
    odd = meta[ODD]
    own_at = odd * count
    either(meta[MOVED], z_came, z_home, lambda own: pltpu.make_async_copy(own, pool.at[pl.ds(own_at, count)], sem).start())
    either(meta[MOVED], mate_a, mate_b, lambda mate: pltpu.make_async_copy(mate, pool.at[pl.ds(count - own_at, count)], sem).start())
    pool[2 * count] = jnp.zeros(pool.shape[1:], pool.dtype)
    for _ in range(2):
        pltpu.make_async_copy(z_home, z_home, sem).wait()
    densify(pool, table, zd, 0, 2 * rows)
    copies = [pltpu.make_async_copy(zd, znear, osem.at[0])]
    copies[0].start()
    own_rows = pl.ds(pl.multiple_of(odd * rows * tile, rows * tile), rows * tile)

    def far_one(i, carry):
        at = pl.ds(pl.multiple_of((odd * 2 * rows + i) * tile, tile), tile)
        zf[pl.ds(pl.multiple_of(i * tile, tile), tile), :] = zd[own_rows, at].T
        return carry

    def own_one(i, carry):
        at = pl.ds(pl.multiple_of((rows + i) * tile, tile), tile)
        zo[pl.ds(pl.multiple_of(i * tile, tile), tile), :] = zd[:, at].T
        return carry

    lax.fori_loop(0, rows, far_one, 0)
    lax.fori_loop(0, rows, own_one, 0)
    copies += [pltpu.make_async_copy(zf, turned_far, osem.at[1]), pltpu.make_async_copy(zo, turned_own, osem.at[2])]
    copies[1].start()
    copies[2].start()
    for copy in copies:
        copy.wait()


def product_kernel(total, rows, half, meta, ftab, ztab, keep, col_of, f_home, f_came, far_a, far_b, far_c, znear, turned, *rest):
    if half:
        earlier, rest = rest[0], rest[1:]
    prod, lent_0, lent_1, packed, fd, zd, pd, zt, fpool, zpool, part, fsem, zsem, tsem, nsem, esem, psem, osem = rest
    count, tile = f_home.shape[:2]
    slots = count // rows
    span, wide = 3 * rows, 2 * H + 2
    base, odd = meta[BASE], meta[ODD]
    few = rows // 2
    here = odd if half == 0 else 1 - odd
    mine = pl.ds(pl.multiple_of(here * few * tile, few * tile), few * tile)
    far_row = jnp.where(odd == 0, 0, 2 * rows)
    near_rows = pl.ds(pl.multiple_of(rows * tile * (1 - odd), rows * tile), 2 * rows * tile)
    f_part = pl.ds(here * (count // 2), count // 2)
    either(
        meta[MOVED], f_came, f_home, lambda fock: pltpu.make_async_copy(fock.at[f_part], fpool.at[: count // 2], fsem).start()
    )
    for kind, far in enumerate((far_b, far_a, far_c)):

        @pl.when(meta[FAR] == kind)
        def _(far=far):
            pltpu.make_async_copy(far, zpool.at[: far.shape[0]], zsem).start()

    near_in = pltpu.make_async_copy(znear, zd.at[near_rows], nsem)
    near_in.start()
    turn_in = pltpu.make_async_copy(turned, zt, tsem)
    turn_in.start()
    if half:
        others = pl.ds(pl.multiple_of(odd * few * tile, few * tile), few * tile)
        early_in = pltpu.make_async_copy(earlier, pd.at[others], esem)
        early_in.start()
    fpool[count // 2] = jnp.zeros(fpool.shape[1:], fpool.dtype)
    zpool[far_a.shape[0]] = jnp.zeros(zpool.shape[1:], zpool.dtype)

    def clear(i, carry):
        at = pl.ds(pl.multiple_of((here * few + i) * tile, tile), tile)
        pd[at, :] = jnp.zeros((tile, pd.shape[1]), pd.dtype)
        return carry

    lax.fori_loop(0, few, clear, 0)
    pltpu.make_async_copy(f_home.at[f_part], fpool.at[: count // 2], fsem).wait()
    densify(fpool, ftab, fd, 0, few)
    pltpu.make_async_copy(far_a, zpool.at[: far_a.shape[0]], zsem).wait()
    densify(zpool, ztab, zd, far_row, rows)
    near_in.wait()
    step = 6 if wide % 6 == 0 else 2
    for q in range(few // 2):
        r = here * (few // 2) + q
        k0 = window(base, rows, r, total)
        kcols = pair_cols(k0, wide, tile)

        def block(nb, carry, q=q, r=r, k0=k0, kcols=kcols):
            first = k0 + step * nb
            acc = jnp.dot(
                fd[2 * q * tile : (2 * q + 2) * tile, kcols],
                zd[kcols, pair_cols(first, step, tile)],
                preferred_element_type=jnp.float32,
            )
            for i in range(2):
                for j in range(step):
                    piece = acc[i * tile : (i + 1) * tile, j * tile : (j + 1) * tile]
                    piece = jnp.where(keep[2 * q + i, first + j] != 0, piece, 0.0)
                    tiles_of(pd, 2 * r + i, first + j, tile)[...] = piece.astype(pd.dtype)
            return carry

        lax.fori_loop(0, wide // step, block, 0)
    writes = [pltpu.make_async_copy(pd.at[mine], prod, psem.at[0])]
    for i, lent in enumerate((lent_0, lent_1)):
        cols = pl.ds(pl.multiple_of((1 - odd + i) * rows * tile, rows * tile), rows * tile)
        writes.append(pltpu.make_async_copy(pd.at[mine, cols], lent, psem.at[1 + i]))
    for write in writes:
        write.start()
    turn_in.wait()
    if half:
        early_in.wait()
    start = jnp.where(odd == 0, 0, rows)
    pairs = rows // 2
    for m in range(half * pairs // 2, (half + 1) * pairs // 2):
        r = jnp.where(odd == 0, m, pairs - 1 - m)
        deep = 2 * (m + 1) * tile
        k_at = pl.ds(pl.multiple_of(jnp.where(odd == 0, 0, rows * tile - deep), 2 * tile), deep)
        n_wide = H + 2 * (m + 1)
        n_at = jnp.where(odd == 0, 0, 2 * H - n_wide)
        acc = jnp.dot(
            zt[pair_rows(2 * r, tile), k_at],
            pd[k_at, pair_cols(start + n_at, n_wide, tile)],
            preferred_element_type=jnp.float32,
        )
        part[pair_rows(2 * r, tile), pair_cols(n_at, n_wide, tile)] = acc.astype(part.dtype)
    low_rows, high_rows = (
        [t for t in pack_order(rows, low, True) for _ in range(widths(slots, rows, low)[t])] for low in (True, False)
    )
    skipped = half * (len(low_rows) - packed.shape[0])
    for p in range(packed.shape[0]):
        t = jnp.where(odd == 1, low_rows[skipped + p], high_rows[skipped + p])
        pltpu.make_async_copy(tiles_of(part, t, col_of[p], tile), packed.at[p], osem).start()
    pltpu.make_async_copy(packed, packed, osem).wait()
    for write in writes:
        write.wait()


def own_kernel(total, rows, meta, col_of, turned, prod_0, prod_1, *rest):
    lent, (near, zt, pd, acc_ref, out, sem, osem) = rest[:-7], rest[-7:]
    count, tile = near.shape[:2]
    slots = count // rows
    base, odd = meta[BASE], meta[ODD]
    wide = 2 * H + 2
    own = rows * tile
    few = own // 2

    def part(index, n):
        return pl.ds(pl.multiple_of(index * own, own), n * own)

    def half_rows(block, index):
        return pl.ds(pl.multiple_of(block * own + index * few, few), few)

    copies = [pltpu.make_async_copy(turned, zt, sem.at[0])]
    for h, prod in enumerate((prod_0, prod_1)):
        mine = half_rows(odd, odd if h == 0 else 1 - odd)
        copies.append(pltpu.make_async_copy(prod, pd.at[mine], sem.at[len(copies)]))
        theirs = half_rows(1 - odd, 1 - odd if h == 0 else odd)
        for i in range(2):
            copies.append(pltpu.make_async_copy(lent[2 * h + i], pd.at[theirs, part(1 - odd + i, 1)], sem.at[len(copies)]))
    for copy in copies:
        copy.start()
    pd[part(1 - odd, 1), part(2 * odd, 1)] = jnp.zeros((own, own), pd.dtype)
    acc_ref[:, 3 * own :] = jnp.zeros((own, tile), acc_ref.dtype)
    for copy in copies:
        copy.wait()
    step = 6 if wide % 6 == 0 else 2
    for r in range(rows // 2):
        k0 = window(base, rows, r, total)

        def block(nb, carry, r=r, k0=k0):
            cols = pair_cols(k0 + step * nb, step, tile)
            acc = jnp.dot(zt[2 * r * tile : (2 * r + 2) * tile, :], pd[:, cols], preferred_element_type=jnp.float32)
            acc_ref[2 * r * tile : (2 * r + 2) * tile, cols] = acc.astype(acc_ref.dtype)
            return carry

        lax.fori_loop(0, wide // step, block, 0)

    def one(t, carry):
        for s in range(slots):
            out[t * slots + s] = tiles_of(acc_ref, t, col_of[t, s], tile)[...]
        return carry

    lax.fori_loop(0, rows, one, 0)
    outward = pltpu.make_async_copy(out, near, osem)
    outward.start()
    outward.wait()


def join_kernel(rows, place, where, near, far_0, far_1, *outs):
    slots = near.shape[0] // rows
    few, tiles = far_0.shape[0], far_0.shape[0] + far_1.shape[0]
    for n, out in enumerate(outs):
        row = where[n]

        def one(s, carry, out=out, row=row):
            at = place[row, s]

            @pl.when(at < few)
            def _():
                out[s] = near[row * slots + s] + far_0[at]

            @pl.when((at >= few) & (at < tiles))
            def _():
                out[s] = near[row * slots + s] + far_1[at - few]

            @pl.when(at >= tiles)
            def _():
                out[s] = near[row * slots + s]

            return carry

        lax.fori_loop(0, slots, one, 0)


def gather_kernel(slot, present, *rest):
    parts, (out, sem) = rest[:-2], rest[-2:]
    for s, part in enumerate(parts):

        @pl.when(present[s] != 0)
        def _(s=s, part=part):
            pltpu.make_async_copy(part, out.at[slot[s]], sem).start()

    pltpu.make_async_copy(out, out, sem).wait()


def call(kernel, scalars, arrays, outs, scratch, name=None, limit=60, cost=1.0, held_in=False, held_out=False):
    any_spec = pl.BlockSpec(memory_space=pl.ANY)
    smem = pl.BlockSpec(memory_space=pltpu.SMEM)
    vmem = pl.BlockSpec(memory_space=pltpu.VMEM)
    return pl.pallas_call(
        kernel,
        in_specs=[smem] * len(scalars) + [vmem if held_in else any_spec] * len(arrays),
        out_specs=[vmem if held_out else any_spec] * len(outs),
        out_shape=outs,
        scratch_shapes=scratch,
        compiler_params=pltpu.CompilerParams(vmem_limit_bytes=limit * 1024 * 1024),
        cost_estimate=pl.CostEstimate(flops=0, bytes_accessed=int(cost * COST_SCALE), transcendentals=0),
        name=name,
    )(*scalars, *arrays)


def body(fock_tiles, fock_pattern, basis_tiles, basis_pattern, product_pattern, result_pattern, new_index):
    rows, slots, tile = fock_tiles.shape[:3]
    total = fock_pattern.shape[0]
    count = rows * slots
    count_rows, count_cols = lax.axis_size("row"), lax.axis_size("col")
    plan = layout(count_rows, count_cols)
    my_row, my_col = lax.axis_index("row"), lax.axis_index("col")
    group = 2 * (my_row // 2) + my_col % 2
    number = 2 * (my_col // 2) + my_row % 2
    block = group * count_cols + number
    base = block * rows
    odd = number % 2
    moved = (my_row + my_col) % 2
    at_edge = ((number == 0) | (number == count_cols - 1)).astype(jnp.int32)
    home = (my_row * count_cols + my_col) * rows
    meta = jnp.stack([jnp.asarray(m, jnp.int32) for m in (base, odd, moved, jnp.where(moved == 1, 1, 2 * at_edge))])
    dtype = fock_tiles.dtype
    packed_tiles = max(sum(widths(slots, rows, side)) for side in (False, True))
    span = 3 * rows

    framed = jnp.pad(
        jnp.concatenate([basis_pattern, result_pattern, fock_pattern, product_pattern], axis=1),
        ((rows, rows), (0, 0)),
        constant_values=-1,
    )
    near = lax.dynamic_slice_in_dim(framed, base, span, 0)
    zpat, rpat, fpat, ppat = (near[:, i * slots : (i + 1) * slots] for i in range(4))
    mid = slice(rows, 2 * rows)
    far_side = jnp.where(odd == 0, jnp.concatenate([zpat, rpat], 1)[:rows], jnp.concatenate([zpat, rpat], 1)[2 * rows :])
    far_base = jnp.where(odd == 0, base - rows, base + rows)
    place, col_of = pack_tables(
        jnp.stack([far_side[:, :slots], far_side[:, slots:], rpat[mid]]),
        jnp.stack([far_base, far_base, base]),
        jnp.stack([odd == 1, odd == 1, odd == 0]),
        (False, True, True),
        packed_tiles,
    )
    origin = base - rows
    slot_ids = jnp.arange(2 * count, dtype=jnp.int32).reshape(2 * rows, slots)
    znear_pat = jnp.where(odd == 0, zpat[rows:], zpat[: 2 * rows])
    near_table = spread(znear_pat, slot_ids, origin, span, 2 * count)
    fock_table = spread(fpat[mid], slot_ids[:rows], origin, span, count)
    far_table = spread(far_side[:, :slots], place[0], origin, span, packed_tiles)
    keep = spread(ppat[mid], jnp.ones((rows, slots), jnp.int32), origin, span, 0)
    far_start = jnp.where(odd == 0, 0, rows)
    far_cols = jnp.clip(col_of[1] - origin - far_start, 0, 2 * H - 1)
    own_cols = jnp.where(rpat[mid] >= 0, rpat[mid] - origin, span)
    own_place = jnp.where(place[2] >= 0, place[2], packed_tiles)

    def permute(x, name):
        return lax.ppermute(x, AXES, plan[name])

    def dense(n_rows, n_cols, kind=dtype):
        return pltpu.VMEM((n_rows * tile, n_cols * tile), kind)

    def pool(n):
        return pltpu.VMEM((n, tile, tile), dtype)

    def shape(*dims):
        return jax.ShapeDtypeStruct(dims, dtype)

    dma = pltpu.SemaphoreType.DMA
    packed_shape = shape(packed_tiles, tile, tile)
    block_shape = shape(count, tile, tile)
    z_home, f_home = basis_tiles.reshape(count, tile, tile), fock_tiles.reshape(count, tile, tile)

    def pack(first, tiles):
        kernel = functools.partial(pack_kernel, rows)
        scalars = [jnp.stack([jnp.asarray(f, jnp.int32) for f in first]), basis_pattern]
        scratch = [pool(count), pltpu.SMEM((packed_tiles + 1,), jnp.int32), dma]
        return call(kernel, scalars, [tiles], [packed_shape], scratch, name="pack", limit=12, cost=4, held_out=True)[0]

    z_came = permute(z_home, "swap")
    mate_a = permute(z_home, "mate_a")
    packed_a = pack((home, my_col % 2), z_home)
    far_a = permute(packed_a, "far_a")
    f_came = permute(f_home, "swap")
    z_came, far_a = lax.optimization_barrier((z_came, far_a))
    far_b = permute(pack((base, odd), z_came), "far_b")
    mate_b = permute(z_came, "mate_b")
    znear, turned_far, turned_own = call(
        functools.partial(near_kernel, rows),
        [meta, near_table],
        [z_home, z_came, mate_a, mate_b],
        [shape(2 * rows * tile, span * tile), shape(rows * tile, rows * tile), shape(rows * tile, 2 * rows * tile)],
        [pool(2 * count + 1), dense(2 * rows, span), dense(rows, rows), dense(rows, 2 * rows), dma, dma((3,))],
        name="near",
        limit=40,
        cost=14,
    )
    packed_a, turned_far = lax.optimization_barrier((packed_a, turned_far))
    far_c = permute(packed_a, "far_c")
    few = sum(widths(slots, rows, False)[: rows // 2])
    half_count, half_rows = count // 2, rows // 2
    prods, lents, fars = [], [], []
    for half in range(2):
        here = odd if half == 0 else 1 - odd
        fock_half = lax.dynamic_slice_in_dim(jnp.where(fock_table == count, count + half_count, fock_table), here * half_rows, half_rows, 0)
        fock_half = jnp.minimum(fock_half - here * half_count, half_count)
        keep_half = lax.dynamic_slice_in_dim(keep, here * half_rows, half_rows, 0)
        tiles_half = few if half == 0 else packed_tiles - few
        prod, lent_0, lent_1, packed = call(
            functools.partial(product_kernel, total, rows, half),
            [meta, fock_half, far_table, keep_half, far_cols[few * half : few * half + tiles_half]],
            [f_home, f_came, far_a, far_b, far_c, znear, turned_far, *prods],
            [shape(half_rows * tile, span * tile)] + [shape(half_rows * tile, rows * tile)] * 2 + [shape(tiles_half, tile, tile)],
            [dense(half_rows, span), dense(span, span), dense(rows, span), dense(rows, rows)]
            + [pool(half_count + 1), pool(packed_tiles + 1), dense(rows, 2 * H)]
            + [dma] * 5
            + [dma((3,)), dma],
            name="product",
            limit=50,
            cost=15,
        )
        if fars:
            packed, fars[0] = lax.optimization_barrier((packed, fars[0]))
        fars.append(permute(packed, "outer"))
        lents += [permute(lent_0, "pair"), permute(lent_1, "pair")]
        prods.append(prod)
    (near_sum,) = call(
        functools.partial(own_kernel, total, rows),
        [meta, own_cols],
        [turned_own, *prods, *lents],
        [block_shape],
        [dense(rows, 2 * rows), dense(2 * rows, span), dense(rows, span + 1), pool(count), dma((7,)), dma],
        name="own",
        limit=40,
        cost=0.1,
    )
    shift = (lax.dynamic_slice_in_dim(new_index, base, rows, 0) // rows - number) % count_cols
    hit = shift[None, :] == jnp.arange(count_cols, dtype=jnp.int32)[:, None]
    where = jnp.sum(hit.astype(jnp.int32) * jnp.arange(rows, dtype=jnp.int32)[None, :], axis=1)
    outs = call(
        functools.partial(join_kernel, rows),
        [own_place, where],
        [near_sum, *fars],
        [shape(slots, tile, tile)] * count_cols,
        [],
        name="join",
        limit=16,
        cost=4,
        held_in=True,
        held_out=True,
    )
    parts = [lax.ppermute(out, AXES, plan["shifts"][s]) for s, out in enumerate(outs)]
    wanted = home + jnp.arange(rows, dtype=jnp.int32)
    found = new_index[None, :] == wanted[:, None]
    anchor = jnp.sum(found.astype(jnp.int32) * jnp.arange(total, dtype=jnp.int32)[None, :], axis=1)
    came = (my_col - anchor // rows) % count_cols
    hit = came[None, :] == jnp.arange(count_cols, dtype=jnp.int32)[:, None]
    slot = jnp.sum(hit.astype(jnp.int32) * jnp.arange(rows, dtype=jnp.int32)[None, :], axis=1)
    present = jnp.sum(hit.astype(jnp.int32), axis=1)
    (out,) = call(
        gather_kernel,
        [slot, present],
        parts,
        [shape(rows, slots, tile, tile)],
        [dma],
        name="gather",
        limit=16,
        cost=3,
        held_in=True,
    )
    return out


def solution(mesh):
    placed = P(AXES, None, None, None)
    return jax.shard_map(
        body,
        mesh=mesh,
        in_specs=(placed, P(), placed, P(), P(), P(), P()),
        out_specs=placed,
        check_vma=False,
    )
```

```python
import functools

import jax
import jax.numpy as jnp
from jax import lax
from jax.experimental import pallas as pl
from jax.experimental.pallas import tpu as pltpu
from jax.sharding import PartitionSpec as P

H = 8
AXES = ("row", "col")
COST_SCALE = 3_000_000


def layout(rows, cols):
    def place(v):
        g, n = divmod(v, cols)
        return (2 * (g // 2) + n % 2) * cols + 2 * (n // 2) + g % 2

    def beside(v):
        return v + 1 if v % 2 else v - 1

    total = rows * cols
    moved = [place(v) != v for v in range(total)]
    edge = [v % cols in (0, cols - 1) for v in range(total)]
    has_outer = [0 <= beside(v) < total for v in range(total)]
    return {
        "swap": [(v, place(v)) for v in range(total) if moved[v]],
        "mate_a": [(place(v), place(v ^ 1)) for v in range(total) if not moved[v]],
        "mate_b": [(place(v), place(v ^ 1)) for v in range(total) if moved[v]],
        "pair": [(place(v), place(v ^ 1)) for v in range(total)],
        "far_a": [(v, place(beside(v))) for v in range(total) if has_outer[v] and moved[v] == edge[v]],
        "far_b": [(place(v), place(beside(v))) for v in range(total) if has_outer[v] and moved[v] and not edge[v]],
        "far_c": [(v, place(beside(v))) for v in range(total) if has_outer[v] and edge[v] and not moved[v]],
        "outer": [(place(v), place(beside(v))) for v in range(total) if has_outer[v]],
        "shifts": [[(place(v), v // cols * cols + (v + s) % cols) for v in range(total)] for s in range(cols)],
    }


BASE, ODD, MOVED, FAR = range(4)


def widths(slots, rows, low):
    return [min(slots, 2 * H - 1 - t if low else H + t) for t in range(rows)]


def pack_order(rows, low, small_first):
    half = rows // 2
    if low and small_first:
        return [*range(half, rows), *range(half)]
    return list(range(rows))


def pack_starts(slots, rows, low, small_first):
    table, starts, at = widths(slots, rows, low), [0] * rows, 0
    for t in pack_order(rows, low, small_first):
        starts[t] = at
        at += table[t]
    return starts


def pack_tables(pattern, base, low, small_first, packed_tiles):
    rows, slots = pattern.shape[1:]
    width = jnp.where(low[:, None], jnp.array(widths(slots, rows, True)), jnp.array(widths(slots, rows, False)))
    starts = [jnp.array([pack_starts(slots, rows, side, first) for first in small_first]) for side in (False, True)]
    offset = jnp.where(low[:, None], starts[1], starts[0])
    beyond = jnp.where(low[:, None, None], pattern <= base[:, None, None] + H - 2, pattern >= base[:, None, None])
    wanted = (pattern >= 0) & beyond
    earlier = jnp.arange(slots)[None, :] < jnp.arange(slots)[:, None]
    rank = jnp.sum((wanted[:, :, None, :] & earlier).astype(jnp.int32), axis=-1)
    place = jnp.where(wanted & (rank < width[:, :, None]), offset[:, :, None] + rank, -1)
    hit = place.reshape(-1, 1, rows * slots) == jnp.arange(packed_tiles)[None, :, None]
    col_of = jnp.max(jnp.where(hit, pattern.reshape(-1, 1, rows * slots), 0), axis=-1)
    return place, col_of


def spread(pattern, values, origin, span, empty):
    at = pattern[:, :, None] - origin == jnp.arange(span)
    found = jnp.max(jnp.where(at & (pattern >= 0)[:, :, None], values[:, :, None], -1), axis=1)
    return jnp.where(found >= 0, found, empty).astype(jnp.int32)


def either(flag, first, second, act):
    @pl.when(flag != 0)
    def _():
        act(first)

    @pl.when(flag == 0)
    def _():
        act(second)


def tiles_of(ref, row, col, tile):
    return ref.at[pl.ds(pl.multiple_of(row * tile, tile), tile), pl.ds(pl.multiple_of(col * tile, tile), tile)]


def pair_cols(first, count, tile):
    return pl.ds(pl.multiple_of(first * tile, 2 * tile), count * tile)


def pair_rows(first, tile):
    return pl.ds(pl.multiple_of(first * tile, 2 * tile), 2 * tile)


def window(base, rows, r, total):
    low = jnp.clip(base + 2 * r - H, 0, total - 2 * H) - (base - rows)
    return jnp.clip(low // 2 * 2, 0, 3 * rows - 2 * H - 2)


def densify(pool, table, dense, row, count):
    tile = pool.shape[1]

    def one(t, carry):
        for c in range(table.shape[1]):
            dense[pl.ds(pl.multiple_of((row + t) * tile, tile), tile), c * tile : (c + 1) * tile] = pool[table[t, c]]
        return carry

    lax.fori_loop(0, count, one, 0)


def pack_kernel(rows, first, pattern, tiles, packed, held, table, sem):
    count = tiles.shape[0]
    slots = count // rows
    inward = pltpu.make_async_copy(tiles, held, sem)
    inward.start()
    start = first[0]
    low = first[1] == 0
    trash = packed.shape[0]
    for p in range(trash):
        table[p] = 0
    tables = [widths(slots, rows, side) for side in (False, True)]
    starts = [[sum(table[:t]) for t in range(rows)] for table in tables]
    for t in range(rows):
        place = jnp.where(low, starts[1][t], starts[0][t])
        end = place + jnp.where(low, tables[1][t], tables[0][t])
        for k in range(slots):
            col = pattern[start + t, k]
            take = (col >= 0) & jnp.where(low, col <= start + H - 2, col >= start) & (place < end)
            table[jnp.where(take, place, trash)] = t * slots + k
            place = place + take.astype(jnp.int32)
    inward.wait()
    for p in range(trash):
        packed[p] = held[table[p]]


def near_kernel(rows, meta, table, z_home, z_came, mate_a, mate_b, znear, turned_far, turned_own, pool, zd, zf, zo, sem, osem):
    count, tile = z_home.shape[:2]
    odd = meta[ODD]
    own_at = odd * count
    either(meta[MOVED], z_came, z_home, lambda own: pltpu.make_async_copy(own, pool.at[pl.ds(own_at, count)], sem).start())
    either(meta[MOVED], mate_a, mate_b, lambda mate: pltpu.make_async_copy(mate, pool.at[pl.ds(count - own_at, count)], sem).start())
    pool[2 * count] = jnp.zeros(pool.shape[1:], pool.dtype)
    for _ in range(2):
        pltpu.make_async_copy(z_home, z_home, sem).wait()
    densify(pool, table, zd, 0, 2 * rows)
    copies = [pltpu.make_async_copy(zd, znear, osem.at[0])]
    copies[0].start()
    own_rows = pl.ds(pl.multiple_of(odd * rows * tile, rows * tile), rows * tile)

    def far_one(i, carry):
        at = pl.ds(pl.multiple_of((odd * 2 * rows + i) * tile, tile), tile)
        zf[pl.ds(pl.multiple_of(i * tile, tile), tile), :] = zd[own_rows, at].T
        return carry

    def own_one(i, carry):
        at = pl.ds(pl.multiple_of((rows + i) * tile, tile), tile)
        zo[pl.ds(pl.multiple_of(i * tile, tile), tile), :] = zd[:, at].T
        return carry

    lax.fori_loop(0, rows, far_one, 0)
    lax.fori_loop(0, rows, own_one, 0)
    copies += [pltpu.make_async_copy(zf, turned_far, osem.at[1]), pltpu.make_async_copy(zo, turned_own, osem.at[2])]
    copies[1].start()
    copies[2].start()
    for copy in copies:
        copy.wait()


def product_kernel(total, rows, half, meta, ftab, ztab, keep, col_of, f_home, f_came, far_a, far_b, far_c, znear, turned, *rest):
    if half:
        earlier, rest = rest[0], rest[1:]
    prod, lent_0, lent_1, packed, fd, zd, pd, zt, fpool, zpool, part, fsem, zsem, tsem, nsem, esem, psem, osem = rest
    count, tile = f_home.shape[:2]
    slots = count // rows
    span, wide = 3 * rows, 2 * H + 2
    base, odd = meta[BASE], meta[ODD]
    few = rows // 2
    here = odd if half == 0 else 1 - odd
    mine = pl.ds(pl.multiple_of(here * few * tile, few * tile), few * tile)
    far_row = jnp.where(odd == 0, 0, 2 * rows)
    near_rows = pl.ds(pl.multiple_of(rows * tile * (1 - odd), rows * tile), 2 * rows * tile)
    f_part = pl.ds(here * (count // 2), count // 2)
    either(
        meta[MOVED], f_came, f_home, lambda fock: pltpu.make_async_copy(fock.at[f_part], fpool.at[: count // 2], fsem).start()
    )
    for kind, far in enumerate((far_b, far_a, far_c)):

        @pl.when(meta[FAR] == kind)
        def _(far=far):
            pltpu.make_async_copy(far, zpool.at[: far.shape[0]], zsem).start()

    near_in = pltpu.make_async_copy(znear, zd.at[near_rows], nsem)
    near_in.start()
    turn_in = pltpu.make_async_copy(turned, zt, tsem)
    turn_in.start()
    if half:
        others = pl.ds(pl.multiple_of(odd * few * tile, few * tile), few * tile)
        early_in = pltpu.make_async_copy(earlier, pd.at[others], esem)
        early_in.start()
    fpool[count // 2] = jnp.zeros(fpool.shape[1:], fpool.dtype)
    zpool[far_a.shape[0]] = jnp.zeros(zpool.shape[1:], zpool.dtype)

    def clear(i, carry):
        at = pl.ds(pl.multiple_of((here * few + i) * tile, tile), tile)
        pd[at, :] = jnp.zeros((tile, pd.shape[1]), pd.dtype)
        return carry

    lax.fori_loop(0, few, clear, 0)
    pltpu.make_async_copy(f_home.at[f_part], fpool.at[: count // 2], fsem).wait()
    densify(fpool, ftab, fd, 0, few)
    pltpu.make_async_copy(far_a, zpool.at[: far_a.shape[0]], zsem).wait()
    densify(zpool, ztab, zd, far_row, rows)
    near_in.wait()
    step = 6 if wide % 6 == 0 else 2
    inner = (base >= 2 * rows) & (base < total - 2 * rows)
    for q in range(few // 2):
        r = here * (few // 2) + q
        k0 = window(base, rows, r, total)

        def block(nb, carry, q=q, r=r, k0=k0, skipped=0, deep=wide):
            first = k0 + step * nb
            kcols = pair_cols(k0 + skipped, deep, tile)
            acc = jnp.dot(
                fd[2 * q * tile : (2 * q + 2) * tile, kcols],
                zd[kcols, pair_cols(first, step, tile)],
                preferred_element_type=jnp.float32,
            )
            for i in range(2):
                for j in range(step):
                    piece = acc[i * tile : (i + 1) * tile, j * tile : (j + 1) * tile]
                    piece = jnp.where(keep[2 * q + i, first + j] != 0, piece, 0.0)
                    tiles_of(pd, 2 * r + i, first + j, tile)[...] = piece.astype(pd.dtype)
            return carry

        @pl.when(inner)
        def _(block=block):
            for nb in range(wide // step):
                low = max(0, step * nb - H + 1) // 2 * 2
                high = min(wide, (step * (nb + 1) + H + 1) // 2 * 2)
                block(nb, 0, skipped=low, deep=high - low)

        @pl.when(jnp.logical_not(inner))
        def _(block=block):
            lax.fori_loop(0, wide // step, block, 0)

    writes = [pltpu.make_async_copy(pd.at[mine], prod, psem.at[0])]
    for i, lent in enumerate((lent_0, lent_1)):
        cols = pl.ds(pl.multiple_of((1 - odd + i) * rows * tile, rows * tile), rows * tile)
        writes.append(pltpu.make_async_copy(pd.at[mine, cols], lent, psem.at[1 + i]))
    for write in writes:
        write.start()
    turn_in.wait()
    if half:
        early_in.wait()
    start = jnp.where(odd == 0, 0, rows)
    pairs = rows // 2
    for m in range(half * pairs // 2, (half + 1) * pairs // 2):
        r = jnp.where(odd == 0, m, pairs - 1 - m)
        deep = 2 * (m + 1) * tile
        k_at = pl.ds(pl.multiple_of(jnp.where(odd == 0, 0, rows * tile - deep), 2 * tile), deep)
        n_wide = H + 2 * (m + 1)
        n_at = jnp.where(odd == 0, 0, 2 * H - n_wide)
        acc = jnp.dot(
            zt[pair_rows(2 * r, tile), k_at],
            pd[k_at, pair_cols(start + n_at, n_wide, tile)],
            preferred_element_type=jnp.float32,
        )
        part[pair_rows(2 * r, tile), pair_cols(n_at, n_wide, tile)] = acc.astype(part.dtype)
    low_rows, high_rows = (
        [t for t in pack_order(rows, low, True) for _ in range(widths(slots, rows, low)[t])] for low in (True, False)
    )
    skipped = half * (len(low_rows) - packed.shape[0])
    for p in range(packed.shape[0]):
        t = jnp.where(odd == 1, low_rows[skipped + p], high_rows[skipped + p])
        pltpu.make_async_copy(tiles_of(part, t, col_of[p], tile), packed.at[p], osem).start()
    pltpu.make_async_copy(packed, packed, osem).wait()
    for write in writes:
        write.wait()


def own_kernel(total, rows, meta, col_of, turned, prod_0, prod_1, *rest):
    lent, (near, zt, pd, acc_ref, out, sem, osem) = rest[:-7], rest[-7:]
    count, tile = near.shape[:2]
    slots = count // rows
    base, odd = meta[BASE], meta[ODD]
    wide = 2 * H + 2
    own = rows * tile
    few = own // 2

    def part(index, n):
        return pl.ds(pl.multiple_of(index * own, own), n * own)

    def half_rows(block, index):
        return pl.ds(pl.multiple_of(block * own + index * few, few), few)

    copies = [pltpu.make_async_copy(turned, zt, sem.at[0])]
    for h, prod in enumerate((prod_0, prod_1)):
        mine = half_rows(odd, odd if h == 0 else 1 - odd)
        copies.append(pltpu.make_async_copy(prod, pd.at[mine], sem.at[len(copies)]))
        theirs = half_rows(1 - odd, 1 - odd if h == 0 else odd)
        for i in range(2):
            copies.append(pltpu.make_async_copy(lent[2 * h + i], pd.at[theirs, part(1 - odd + i, 1)], sem.at[len(copies)]))
    for copy in copies:
        copy.start()
    pd[part(1 - odd, 1), part(2 * odd, 1)] = jnp.zeros((own, own), pd.dtype)
    acc_ref[:, 3 * own :] = jnp.zeros((own, tile), acc_ref.dtype)
    for copy in copies:
        copy.wait()
    step = 6 if wide % 6 == 0 else 2
    inner = (base >= 2 * rows) & (base < total - 2 * rows)
    for m in range(rows // 2):
        r = jnp.where(odd == 0, m, rows // 2 - 1 - m)
        k0 = window(base, rows, r, total)

        def block(nb, carry, r=r, k0=k0, deep=2 * rows):
            cols = pair_cols(k0 + step * nb, step, tile)
            k_at = pl.ds(pl.multiple_of(jnp.where(odd == 0, 0, 2 * rows - deep) * tile, 2 * tile), deep * tile)
            acc = jnp.dot(zt[pair_rows(2 * r, tile), k_at], pd[k_at, cols], preferred_element_type=jnp.float32)
            acc_ref[pair_rows(2 * r, tile), cols] = acc.astype(acc_ref.dtype)
            return carry

        @pl.when(inner)
        def _(block=block, m=m):
            lax.fori_loop(0, wide // step, functools.partial(block, deep=min(2 * rows, 2 * m + H + 2)), 0)

        @pl.when(jnp.logical_not(inner))
        def _(block=block):
            lax.fori_loop(0, wide // step, block, 0)


    def one(t, carry):
        for s in range(slots):
            out[t * slots + s] = tiles_of(acc_ref, t, col_of[t, s], tile)[...]
        return carry

    lax.fori_loop(0, rows, one, 0)
    outward = pltpu.make_async_copy(out, near, osem)
    outward.start()
    outward.wait()


def join_kernel(rows, place, where, near, far_0, far_1, *outs):
    slots = near.shape[0] // rows
    few, tiles = far_0.shape[0], far_0.shape[0] + far_1.shape[0]
    for n, out in enumerate(outs):
        row = where[n]

        def one(s, carry, out=out, row=row):
            at = place[row, s]

            @pl.when(at < few)
            def _():
                out[s] = near[row * slots + s] + far_0[at]

            @pl.when((at >= few) & (at < tiles))
            def _():
                out[s] = near[row * slots + s] + far_1[at - few]

            @pl.when(at >= tiles)
            def _():
                out[s] = near[row * slots + s]

            return carry

        lax.fori_loop(0, slots, one, 0)


def gather_kernel(slot, present, *rest):
    parts, (out, sem) = rest[:-2], rest[-2:]
    for s, part in enumerate(parts):

        @pl.when(present[s] != 0)
        def _(s=s, part=part):
            pltpu.make_async_copy(part, out.at[slot[s]], sem).start()

    pltpu.make_async_copy(out, out, sem).wait()


def call(kernel, scalars, arrays, outs, scratch, name=None, limit=60, cost=1.0, held_in=False, held_out=False):
    any_spec = pl.BlockSpec(memory_space=pl.ANY)
    smem = pl.BlockSpec(memory_space=pltpu.SMEM)
    vmem = pl.BlockSpec(memory_space=pltpu.VMEM)
    return pl.pallas_call(
        kernel,
        in_specs=[smem] * len(scalars) + [vmem if held_in else any_spec] * len(arrays),
        out_specs=[vmem if held_out else any_spec] * len(outs),
        out_shape=outs,
        scratch_shapes=scratch,
        compiler_params=pltpu.CompilerParams(vmem_limit_bytes=limit * 1024 * 1024),
        cost_estimate=pl.CostEstimate(flops=0, bytes_accessed=int(cost * COST_SCALE), transcendentals=0),
        name=name,
    )(*scalars, *arrays)


def body(fock_tiles, fock_pattern, basis_tiles, basis_pattern, product_pattern, result_pattern, new_index):
    rows, slots, tile = fock_tiles.shape[:3]
    total = fock_pattern.shape[0]
    count = rows * slots
    count_rows, count_cols = lax.axis_size("row"), lax.axis_size("col")
    plan = layout(count_rows, count_cols)
    my_row, my_col = lax.axis_index("row"), lax.axis_index("col")
    group = 2 * (my_row // 2) + my_col % 2
    number = 2 * (my_col // 2) + my_row % 2
    block = group * count_cols + number
    base = block * rows
    odd = number % 2
    moved = (my_row + my_col) % 2
    at_edge = ((number == 0) | (number == count_cols - 1)).astype(jnp.int32)
    home = (my_row * count_cols + my_col) * rows
    meta = jnp.stack([jnp.asarray(m, jnp.int32) for m in (base, odd, moved, jnp.where(moved == 1, 1, 2 * at_edge))])
    dtype = fock_tiles.dtype
    packed_tiles = max(sum(widths(slots, rows, side)) for side in (False, True))
    span = 3 * rows

    framed = jnp.pad(
        jnp.concatenate([basis_pattern, result_pattern, fock_pattern, product_pattern], axis=1),
        ((rows, rows), (0, 0)),
        constant_values=-1,
    )
    near = lax.dynamic_slice_in_dim(framed, base, span, 0)
    zpat, rpat, fpat, ppat = (near[:, i * slots : (i + 1) * slots] for i in range(4))
    mid = slice(rows, 2 * rows)
    far_side = jnp.where(odd == 0, jnp.concatenate([zpat, rpat], 1)[:rows], jnp.concatenate([zpat, rpat], 1)[2 * rows :])
    far_base = jnp.where(odd == 0, base - rows, base + rows)
    place, col_of = pack_tables(
        jnp.stack([far_side[:, :slots], far_side[:, slots:], rpat[mid]]),
        jnp.stack([far_base, far_base, base]),
        jnp.stack([odd == 1, odd == 1, odd == 0]),
        (False, True, True),
        packed_tiles,
    )
    origin = base - rows
    slot_ids = jnp.arange(2 * count, dtype=jnp.int32).reshape(2 * rows, slots)
    znear_pat = jnp.where(odd == 0, zpat[rows:], zpat[: 2 * rows])
    near_table = spread(znear_pat, slot_ids, origin, span, 2 * count)
    fock_table = spread(fpat[mid], slot_ids[:rows], origin, span, count)
    far_table = spread(far_side[:, :slots], place[0], origin, span, packed_tiles)
    keep = spread(ppat[mid], jnp.ones((rows, slots), jnp.int32), origin, span, 0)
    far_start = jnp.where(odd == 0, 0, rows)
    far_cols = jnp.clip(col_of[1] - origin - far_start, 0, 2 * H - 1)
    own_cols = jnp.where(rpat[mid] >= 0, rpat[mid] - origin, span)
    own_place = jnp.where(place[2] >= 0, place[2], packed_tiles)

    def permute(x, name):
        return lax.ppermute(x, AXES, plan[name])

    def dense(n_rows, n_cols, kind=dtype):
        return pltpu.VMEM((n_rows * tile, n_cols * tile), kind)

    def pool(n):
        return pltpu.VMEM((n, tile, tile), dtype)

    def shape(*dims):
        return jax.ShapeDtypeStruct(dims, dtype)

    dma = pltpu.SemaphoreType.DMA
    packed_shape = shape(packed_tiles, tile, tile)
    block_shape = shape(count, tile, tile)
    z_home, f_home = basis_tiles.reshape(count, tile, tile), fock_tiles.reshape(count, tile, tile)

    def pack(first, tiles):
        kernel = functools.partial(pack_kernel, rows)
        scalars = [jnp.stack([jnp.asarray(f, jnp.int32) for f in first]), basis_pattern]
        scratch = [pool(count), pltpu.SMEM((packed_tiles + 1,), jnp.int32), dma]
        return call(kernel, scalars, [tiles], [packed_shape], scratch, name="pack", limit=12, cost=4, held_out=True)[0]

    z_came = permute(z_home, "swap")
    mate_a = permute(z_home, "mate_a")
    packed_a = pack((home, my_col % 2), z_home)
    far_a = permute(packed_a, "far_a")
    f_came = permute(f_home, "swap")
    z_came, far_a = lax.optimization_barrier((z_came, far_a))
    far_b = permute(pack((base, odd), z_came), "far_b")
    mate_b = permute(z_came, "mate_b")
    znear, turned_far, turned_own = call(
        functools.partial(near_kernel, rows),
        [meta, near_table],
        [z_home, z_came, mate_a, mate_b],
        [shape(2 * rows * tile, span * tile), shape(rows * tile, rows * tile), shape(rows * tile, 2 * rows * tile)],
        [pool(2 * count + 1), dense(2 * rows, span), dense(rows, rows), dense(rows, 2 * rows), dma, dma((3,))],
        name="near",
        limit=40,
        cost=14,
    )
    packed_a, turned_far = lax.optimization_barrier((packed_a, turned_far))
    far_c = permute(packed_a, "far_c")
    few = sum(widths(slots, rows, False)[: rows // 2])
    half_count, half_rows = count // 2, rows // 2
    prods, lents, fars = [], [], []
    for half in range(2):
        here = odd if half == 0 else 1 - odd
        fock_half = lax.dynamic_slice_in_dim(jnp.where(fock_table == count, count + half_count, fock_table), here * half_rows, half_rows, 0)
        fock_half = jnp.minimum(fock_half - here * half_count, half_count)
        keep_half = lax.dynamic_slice_in_dim(keep, here * half_rows, half_rows, 0)
        tiles_half = few if half == 0 else packed_tiles - few
        prod, lent_0, lent_1, packed = call(
            functools.partial(product_kernel, total, rows, half),
            [meta, fock_half, far_table, keep_half, far_cols[few * half : few * half + tiles_half]],
            [f_home, f_came, far_a, far_b, far_c, znear, turned_far, *prods],
            [shape(half_rows * tile, span * tile)] + [shape(half_rows * tile, rows * tile)] * 2 + [shape(tiles_half, tile, tile)],
            [dense(half_rows, span), dense(span, span), dense(rows, span), dense(rows, rows)]
            + [pool(half_count + 1), pool(packed_tiles + 1), dense(rows, 2 * H)]
            + [dma] * 5
            + [dma((3,)), dma],
            name="product",
            limit=50,
            cost=15,
        )
        if fars:
            packed, fars[0] = lax.optimization_barrier((packed, fars[0]))
        fars.append(permute(packed, "outer"))
        lents += [permute(lent_0, "pair"), permute(lent_1, "pair")]
        prods.append(prod)
    (near_sum,) = call(
        functools.partial(own_kernel, total, rows),
        [meta, own_cols],
        [turned_own, *prods, *lents],
        [block_shape],
        [dense(rows, 2 * rows), dense(2 * rows, span), dense(rows, span + 1), pool(count), dma((7,)), dma],
        name="own",
        limit=40,
        cost=0.1,
    )
    shift = (lax.dynamic_slice_in_dim(new_index, base, rows, 0) // rows - number) % count_cols
    hit = shift[None, :] == jnp.arange(count_cols, dtype=jnp.int32)[:, None]
    where = jnp.sum(hit.astype(jnp.int32) * jnp.arange(rows, dtype=jnp.int32)[None, :], axis=1)
    outs = call(
        functools.partial(join_kernel, rows),
        [own_place, where],
        [near_sum, *fars],
        [shape(slots, tile, tile)] * count_cols,
        [],
        name="join",
        limit=16,
        cost=4,
        held_in=True,
        held_out=True,
    )
    parts = [lax.ppermute(out, AXES, plan["shifts"][s]) for s, out in enumerate(outs)]
    wanted = home + jnp.arange(rows, dtype=jnp.int32)
    found = new_index[None, :] == wanted[:, None]
    anchor = jnp.sum(found.astype(jnp.int32) * jnp.arange(total, dtype=jnp.int32)[None, :], axis=1)
    came = (my_col - anchor // rows) % count_cols
    hit = came[None, :] == jnp.arange(count_cols, dtype=jnp.int32)[:, None]
    slot = jnp.sum(hit.astype(jnp.int32) * jnp.arange(rows, dtype=jnp.int32)[None, :], axis=1)
    present = jnp.sum(hit.astype(jnp.int32), axis=1)
    (out,) = call(
        gather_kernel,
        [slot, present],
        parts,
        [shape(rows, slots, tile, tile)],
        [dma],
        name="gather",
        limit=16,
        cost=3,
        held_in=True,
    )
    return out


def solution(mesh):
    placed = P(AXES, None, None, None)
    return jax.shard_map(
        body,
        mesh=mesh,
        in_specs=(placed, P(), placed, P(), P(), P(), P()),
        out_specs=placed,
        check_vma=False,
    )
```
